128 devices in a mesh: head: 8 (over x, core), expert: 16 (over z, y).
Axes of the slice: x: 4, y: 4, z: 4, core: 2. Of those that a mesh axis runs over, the one named last changes fastest.
Arguments:
- queries: bfloat16 [16, 128, 6144], P('expert', None, 'head')
- key_states: bfloat16 [16, 128, 1024], P('expert', None, 'head')
- corrupted_value_state: bfloat16 [16, 128, 1024], P('expert', None, 'head'), may hold values from -6 to 6
- clean_heads: bfloat16 [16, 128, 6144], P('expert', None, 'head'), may hold values from -6 to 6
- patch_heads: int32 [16, 8], P('expert'), may hold values from 0 to 47, as said below
- out_weight: bfloat16 [6144, 6144], P('head', 'expert'), may hold values from -0.078125 to 0.078125
- residual: bfloat16 [16, 128, 6144], P('expert', 'head'), may hold values from -6 to 6
- norm_gain: float32 [6144], replicated, may hold values from 0.1 to 1.9
- expert_ids: int32 [16, 128, 2], P('expert', 'head'), may hold values from 0 to 7, all different within a row; in each aligned block of 16 rows (0 to 15, 16 to 31, ..., all dimensions but the last counted through in order) at most 6 rows name the same one
- route_weights: float32 [16, 128, 2], P('expert', 'head'), may hold values from 0.1 to 0.9
- gate_weight: bfloat16 [8, 6144, 8192], P('head', None, 'expert'), may hold values from -0.078125 to 0.078125
- up_weight: bfloat16 [8, 6144, 8192], P('head', None, 'expert'), may hold values from -0.078125 to 0.078125
- down_weight: bfloat16 [8, 8192, 6144], P('head', 'expert'), may hold values from -0.0625 to 0.0625
Outputs:
- layer_out: bfloat16 [16, 128, 6144], P('expert', 'head')
The draws below stay inside these ranges and needn't reach their ends.
Inputs may be any that keep to these rules, and one draw needn't show every extreme that they name: `expert_ids`: each row names 2 different experts; among the rows of one device (aligned blocks of 16 positions of a prompt) no expert is named more than 6 times, and 6 is reached. `patch_heads`: each row names 8 different heads.
All inputs are finite; a program needn't handle non-finite values.
Results may differ from the reference program's by a relative error of at most 0.023.
Values may be sent and summed in bfloat16 or wider, within the bound.
No kernel may reach another device: no remote copies, remote signals or barrier semaphores. Data moves between devices by JAX's collectives and lax.ppermute only.
A program may use at most 128 MiB of HBM per device.

```python
import math
import jax
import jax.numpy as jnp
import numpy as np
from jax import lax

D = 6144
QUERY_HEADS = 48
KEY_VALUE_HEADS = 8
HEAD_SIZE = 128
FF = 8192
TOP = 2
NPATCH = 8
PROMPT_LENGTH = 128
EXPERTS = 8
PROMPT_COUNT = 16
TOKS = 16
CAP = 6
QGROUP = 768
FSLICE = 512
N_HEAD = 8
N_EXPERT = 16


def shared_keys(key):
    return jnp.clip(jax.random.normal(jax.random.fold_in(key, 101), (PROMPT_COUNT, PROMPT_LENGTH, KEY_VALUE_HEADS * HEAD_SIZE), jnp.float32), -6.0, 6.0)


def draw_key_states(key, part):
    baseline_run = shared_keys(key)
    return baseline_run.astype(jnp.bfloat16)


def draw_queries(key, part):
    key = jax.random.fold_in(key, 5)
    fresh = jnp.clip(jax.random.normal(key, (PROMPT_COUNT, PROMPT_LENGTH, QUERY_HEADS * HEAD_SIZE), jnp.float32), -6.0, 6.0)
    return fresh.astype(jnp.bfloat16)


def draw_patch_heads(key, part):
    key = jax.random.fold_in(key, 7)
    heads = jnp.arange(QUERY_HEADS).astype(jnp.int32)[None, :]
    prompts = jnp.arange(PROMPT_COUNT).astype(jnp.int32)[:, None]
    scores = jax.random.randint(key, (PROMPT_COUNT, QUERY_HEADS), 0, 1 << 20) * QUERY_HEADS + heads
    favored = (prompts == 0) & (heads == QUERY_HEADS - 1) | (prompts == PROMPT_COUNT - 1) & (heads == 0)
    scores = scores + favored.astype(jnp.int32) * (QUERY_HEADS << 20)
    unused, picked = lax.top_k(scores, NPATCH)
    return picked.astype(jnp.int32)


def levels(stream_key, extent, split, smallest, largest):
    def one(axis_at, blocks):
        draws = jax.random.uniform(jax.random.fold_in(jax.random.fold_in(stream_key, 6), axis_at), (blocks,), jnp.float32, smallest / len(split), largest / len(split))
        return jnp.repeat(jnp.exp(draws), extent[axis_at] // blocks).reshape((-1,) + (1,) * (len(extent) - axis_at - 1))

    loudness = one(*split[0])
    for cut in split[1:]:
        loudness = loudness * one(*cut)
    return loudness


def shared_out(key, own, number, rows, number_of, top, limit, slope):
    ranking = jax.random.permutation(key, number_of)
    heavy_load, ordinary = portions_of(number_of, rows * top, limit, slope, True), portions_of(number_of, rows * top, limit, slope, False)
    places = jnp.arange(number_of)

    def named(lengths, turn):
        used = int((lengths > 0).sum())
        fixed = max(1, used // 4)
        moved = fixed + (places - fixed + turn * (used - fixed)) % max(1, number_of - fixed)
        return jnp.zeros((number_of,), jnp.int32).at[ranking[jnp.where(places < fixed, places, moved)]].set(jnp.asarray(lengths, jnp.int32))

    lengths = jnp.where(number % 4 == 0, named(heavy_load, number // 4), named(ordinary, number - number // 4 - 1))
    mixed = jax.random.permutation(jax.random.fold_in(own, 3), number_of)
    donor, receiver = mixed[0:number_of // 2 * 2:2], mixed[1:number_of // 2 * 2:2]
    room = jnp.minimum(lengths[donor] - 1, limit - lengths[receiver]) // 2
    room = jnp.where((donor == ranking[0]) | (receiver == ranking[0]) | (lengths[receiver] == 0), 0, jnp.maximum(room, 0))
    moved = jax.random.randint(jax.random.fold_in(own, 4), (number_of // 2,), 0, 1 << 20) % (room + 1)
    lengths = lengths.at[donor].add(-moved).at[receiver].add(moved)
    items = jnp.searchsorted(jnp.cumsum(lengths), jnp.arange(rows * top), side="right").astype(jnp.int32)
    table = items.reshape(top, rows).T
    table = table[jax.random.permutation(jax.random.fold_in(own, 1), rows)]
    turn = jax.random.randint(jax.random.fold_in(own, 2), (rows, 1), 0, top)
    return jnp.take_along_axis(table, (jnp.arange(top)[None, :] + turn) % top, axis=1)


def portions_of(amount, total, bound, lean, full):
    weights = [(1 << 20) // math.isqrt(standing ** lean) + 1 for standing in range(1, amount + 1)]
    largest = bound if full else min(bound, max(-(-total // amount), total * weights[0] // sum(weights)))
    least = 1 if total - largest >= amount - 1 else 0
    given, surplus = [largest] + [least] * (amount - 1), total - largest - least * (amount - 1)
    while surplus > 0:
        candidates = [i for i in range(1, amount) if given[i] < largest] or [i for i in range(1, amount) if given[i] < bound]
        pool, budget = sum([weights[i] for i in candidates]), surplus
        for i in candidates:
            extra = min(bound - given[i], max(1, budget * weights[i] // pool), surplus)
            given[i] = given[i] + extra
            surplus = surplus - extra
    return np.array(given)


def noise(stream_key, shape, spread, most, cuts=(), held_as=jnp.bfloat16):
    array = spread * jax.random.normal(stream_key, shape, jnp.float32)
    if cuts:
        array = array * levels(stream_key, shape, cuts, -0.22, 0.18)
    return jnp.clip(array, -most, most).astype(held_as)


def setup_inputs(seed: int = 0) -> dict:
    arg_keys = jax.random.split(jax.random.key(seed), 14)
    queries = draw_queries(jax.random.fold_in(arg_keys[13], 71), 0)
    key_states = draw_key_states(jax.random.fold_in(arg_keys[13], 71), 0)
    corrupted_value_state = noise(arg_keys[2], (PROMPT_COUNT, PROMPT_LENGTH, KEY_VALUE_HEADS * HEAD_SIZE), 2.0, 6.0, ((0, 16), (2, 8)))
    clean_heads = noise(arg_keys[3], (PROMPT_COUNT, PROMPT_LENGTH, QUERY_HEADS * HEAD_SIZE), 0.5, 6.0, ((0, 16), (2, 8)))
    patch_heads = draw_patch_heads(jax.random.fold_in(arg_keys[13], 71), 0)
    out_weight = noise(arg_keys[5], (QUERY_HEADS * HEAD_SIZE, D), (QUERY_HEADS * HEAD_SIZE) ** -0.5, 0.078125, ((0, 8), (1, 16)))
    residual = noise(arg_keys[6], (PROMPT_COUNT, PROMPT_LENGTH, D), 0.5, 6.0, ((0, 16), (1, 8)))
    norm_gain = jnp.clip(1.0 + 0.18 * jax.random.normal(arg_keys[7], (D,), jnp.float32), 0.1, 1.9)
    expert_ids_keys = jax.random.split(jax.random.fold_in(arg_keys[8], 1), PROMPT_COUNT * PROMPT_LENGTH // TOKS)
    expert_ids_turns = jax.random.permutation(jax.random.fold_in(arg_keys[8], 3), PROMPT_COUNT * PROMPT_LENGTH // TOKS)
    expert_ids = jax.vmap(lambda own, number: shared_out(jax.random.fold_in(arg_keys[8], 2), own, number, TOKS, EXPERTS, TOP, CAP, 1))(expert_ids_keys, expert_ids_turns).reshape((PROMPT_COUNT, PROMPT_LENGTH, TOP))
    route_weights = jnp.clip(0.1 + 0.79999997 * jax.random.uniform(arg_keys[9], (PROMPT_COUNT, PROMPT_LENGTH, TOP), jnp.float32) ** levels(arg_keys[9], (PROMPT_COUNT, PROMPT_LENGTH, TOP), ((0, 16), (1, 8)), -0.2, 0.2), 0.1, 0.9)
    gate_weight = noise(arg_keys[10], (EXPERTS, D, FF), D ** -0.5, 0.078125, ((0, 8), (2, 16)))
    up_weight = noise(arg_keys[11], (EXPERTS, D, FF), D ** -0.5, 0.078125, ((0, 8), (2, 16)))
    down_weight = noise(arg_keys[12], (EXPERTS, FF, D), FF ** -0.5, 0.0625, ((0, 8), (1, 16)))
    return {"queries": queries, "key_states": key_states, "corrupted_value_state": corrupted_value_state, "clean_heads": clean_heads, "patch_heads": patch_heads, "out_weight": out_weight, "residual": residual, "norm_gain": norm_gain, "expert_ids": expert_ids, "route_weights": route_weights, "gate_weight": gate_weight, "up_weight": up_weight, "down_weight": down_weight}


def reference(queries, key_states, corrupted_value_state, clean_heads, patch_heads, out_weight, residual, norm_gain, expert_ids, route_weights, gate_weight, up_weight, down_weight):
    scale = 1.0 / math.sqrt(HEAD_SIZE)
    query_groups = QUERY_HEADS // KEY_VALUE_HEADS
    places = jnp.arange(PROMPT_LENGTH)
    causal = places[:, None] >= places[None, :]

    def attend(inputs):
        query_matrix, key_matrix, value_matrix = inputs
        query_tensor = query_matrix.astype(jnp.float32).reshape(PROMPT_LENGTH, KEY_VALUE_HEADS, query_groups, HEAD_SIZE)
        key_cube = key_matrix.astype(jnp.float32).reshape(PROMPT_LENGTH, KEY_VALUE_HEADS, HEAD_SIZE)
        value_cube = value_matrix.astype(jnp.float32).reshape(PROMPT_LENGTH, KEY_VALUE_HEADS, HEAD_SIZE)
        scores = jnp.einsum('igjd,tgd->gjit', query_tensor, key_cube) * scale
        scores = jnp.where(causal[None, None], scores, -jnp.inf)
        highest = lax.optimization_barrier(jnp.max(scores, axis=-1, keepdims=True))
        raised = jnp.exp(scores - highest)
        probs = (raised / lax.optimization_barrier(jnp.sum(raised, axis=-1, keepdims=True))).astype(jnp.bfloat16)
        mixed_values = jnp.einsum('gjit,tgd->igjd', probs.astype(jnp.float32), value_cube)
        return mixed_values.astype(jnp.bfloat16).reshape(PROMPT_LENGTH, QUERY_HEADS * HEAD_SIZE)
    attended = lax.map(attend, (queries, key_states, corrupted_value_state))
    head_numbers = jnp.arange(QUERY_HEADS).astype(jnp.int32)
    chosen = jnp.any(patch_heads[:, :, None] == head_numbers[None, None, :], axis=1)
    merged = jnp.where(chosen[:, None, :, None], clean_heads.reshape(PROMPT_COUNT, PROMPT_LENGTH, QUERY_HEADS, HEAD_SIZE), attended.reshape(PROMPT_COUNT, PROMPT_LENGTH, QUERY_HEADS, HEAD_SIZE))
    merged_rows = merged.reshape(PROMPT_COUNT * PROMPT_LENGTH, QUERY_HEADS * HEAD_SIZE)
    projected = jnp.zeros((PROMPT_COUNT * PROMPT_LENGTH, D), jnp.float32)
    for group_index in range(N_HEAD):
        lower = group_index * QGROUP
        partial_sum = jnp.dot(merged_rows[:, lower:lower + QGROUP], out_weight[lower:lower + QGROUP], preferred_element_type=jnp.float32)
        rounded = lax.optimization_barrier(partial_sum.astype(jnp.bfloat16))
        projected = projected + rounded.astype(jnp.float32)
    hidden_in = residual.reshape(PROMPT_COUNT * PROMPT_LENGTH, D).astype(jnp.float32) + projected
    mean_square = lax.optimization_barrier(jnp.mean(hidden_in * hidden_in, axis=-1, keepdims=True))
    expert_in = (hidden_in * lax.rsqrt(mean_square + 1e-05) * norm_gain).astype(jnp.bfloat16)
    blocks = PROMPT_COUNT * N_HEAD
    pairs = expert_ids.reshape(blocks, TOKS * TOP).astype(jnp.int32)
    expert_numbers = jnp.arange(EXPERTS).astype(jnp.int32)
    onehot_pairs = (pairs[:, :, None] == expert_numbers[None, None, :]).astype(jnp.int32)
    ranks = lax.optimization_barrier(jnp.sum(onehot_pairs * (jnp.cumsum(onehot_pairs, axis=1) - 1), axis=2)).astype(jnp.int32)
    block_numbers = jnp.arange(blocks).astype(jnp.int32)
    slot_index = (block_numbers[:, None] * CAP + ranks).reshape(-1).astype(jnp.int32)
    pair_experts = pairs.reshape(-1)
    pair_rows = jnp.repeat(expert_in, TOP, axis=0)
    buffers = jnp.zeros((EXPERTS, blocks * CAP, D), jnp.bfloat16).at[pair_experts, slot_index].set(pair_rows)

    def run_expert(inputs):
        rows, gate_block, up_block, down_block = inputs
        gate_act = jnp.dot(rows, gate_block, preferred_element_type=jnp.float32)
        up_act = jnp.dot(rows, up_block, preferred_element_type=jnp.float32)
        hidden = (jax.nn.silu(gate_act) * up_act).astype(jnp.bfloat16)
        hidden_pieces = hidden.reshape(rows.shape[0], N_EXPERT, FSLICE).transpose(1, 0, 2)
        down_pieces = down_block.reshape(N_EXPERT, FSLICE, D)

        def add_slice(total, pieces):
            hidden_piece, down_piece = pieces
            term = jnp.dot(hidden_piece, down_piece, preferred_element_type=jnp.float32)
            term_rounded = lax.optimization_barrier(term.astype(jnp.bfloat16))
            return (total + term_rounded.astype(jnp.float32), None)
        total, unused = lax.scan(add_slice, jnp.zeros((rows.shape[0], D), jnp.float32), (hidden_pieces, down_pieces))
        return total.astype(jnp.bfloat16)
    outputs = lax.map(run_expert, (buffers, gate_weight, up_weight, down_weight))
    picked = outputs[pair_experts, slot_index].astype(jnp.float32)
    weighted = picked * route_weights.reshape(-1)[:, None]
    mixture = lax.optimization_barrier(jnp.sum(weighted.reshape(PROMPT_COUNT * PROMPT_LENGTH, TOP, D), axis=1))
    return (hidden_in + mixture).astype(jnp.bfloat16).reshape(PROMPT_COUNT, PROMPT_LENGTH, D)
```

```python
import math

import jax
import jax.numpy as jnp
from jax import lax
from jax.experimental import pallas as pl
from jax.experimental.pallas import tpu as pltpu
from jax.sharding import PartitionSpec as P

HEAD_SIZE = 128
RING = 4
NEAR_FIRST = (0, -1, 1, 2)
FAR_FIRST = (2, 1, -1, 0)
BF = jnp.bfloat16
F32 = jnp.float32


def z_pairs(step):
    return [(z * RING + y, ((z + step) % RING) * RING + y) for z in range(RING) for y in range(RING)]


def y_pairs(step):
    return [(z * RING + y, z * RING + (y + step) % RING) for z in range(RING) for y in range(RING)]


def send(block, pairs):
    return lax.ppermute(block, "expert", pairs)


def gather_near(block, pairs):
    half = block.shape[0] // 2
    up = send(block, pairs(1))
    down = send(block, pairs(-1))
    far_low = send(up[:half], pairs(1))
    far_high = send(down[half:], pairs(-1))
    return jnp.stack([block, up, down, jnp.concatenate([far_low, far_high], axis=0)])


def gather_far(stack, pairs):
    half = RING // 2
    up = send(stack, pairs(1))
    down = send(stack, pairs(-1))
    far_low = send(up[:half], pairs(1))
    far_high = send(down[half:], pairs(-1))
    return [stack, up, down, far_low, far_high]


def gather_two(first, second):
    first_stack = gather_near(first, z_pairs)
    second_stack = gather_near(second, y_pairs)
    return gather_far(first_stack, y_pairs), gather_far(second_stack, z_pairs)


def ring_sum(far, plus, minus, own, pairs, axis):
    size = far.shape[axis]
    far_low = lax.slice_in_dim(far, 0, size // 2, axis=axis)
    far_high = lax.slice_in_dim(far, size // 2, size, axis=axis)
    from_minus = send(far_low, pairs(1))
    from_plus = send(far_high, pairs(-1))

    def add(low, high):
        return (low.astype(F32) + high.astype(F32)).astype(BF)

    plus_low = add(lax.slice_in_dim(plus, 0, size // 2, axis=axis), from_minus)
    plus_all = jnp.concatenate(
        [plus_low, lax.slice_in_dim(plus, size // 2, size, axis=axis)], axis=axis
    )
    minus_high = add(lax.slice_in_dim(minus, size // 2, size, axis=axis), from_plus)
    minus_all = jnp.concatenate(
        [lax.slice_in_dim(minus, 0, size // 2, axis=axis), minus_high], axis=axis
    )
    above = send(plus_all, pairs(1))
    below = send(minus_all, pairs(-1))
    return (own.astype(F32) + above.astype(F32) + below.astype(F32)).astype(BF)


def project_kernel(
    place_a, place_b, a0, a1, a2, a3, a4, b0, b1, b2, b3, b4, weight, resid, gain, targets,
    projected, slots, sum_a, sum_b, rows,
):
    half_groups = a0.shape[1]
    count = projected.shape[0]
    for refs, total, base in (
        ((a0, a1, a2, a3, a4), sum_a, 0),
        ((b0, b1, b2, b3, b4), sum_b, half_groups),
    ):
        acc = None
        for group in range(half_groups):
            pieces = [ref[:, group] for ref in refs]
            block = jnp.concatenate(pieces, axis=0)
            block = block.reshape(-1, block.shape[-1])
            term = jnp.dot(block, weight[base + group], preferred_element_type=F32)
            acc = term if acc is None else acc + term
        total[...] = acc.reshape(total.shape)
    width = projected.shape[2]
    for prompt in range(count):
        value = sum_a[place_a[prompt]] + sum_b[place_b[prompt]]
        projected[prompt] = value.astype(BF)
        hidden = value + resid[prompt][:, :width].astype(F32)
        rows[prompt] = (hidden * gain[...]).astype(BF)
    tokens = rows[...].reshape(-1, width)
    slot_ids = lax.broadcasted_iota(jnp.int32, (slots.shape[0], tokens.shape[0]), 0)
    chosen = (slot_ids == targets[0:1, :]) | (slot_ids == targets[1:2, :])
    dispatch = jnp.where(chosen, 1.0, 0.0).astype(BF)
    slots[...] = jnp.dot(dispatch, tokens, preferred_element_type=F32).astype(BF)


def project(place_a, place_b, first, second, weight, resid, gain, targets, slot_count):
    count, rows = resid.shape[0], resid.shape[1]
    width = weight.shape[2]
    whole = pl.BlockSpec(memory_space=pltpu.VMEM)
    return pl.pallas_call(
        project_kernel,
        out_shape=[
            jax.ShapeDtypeStruct((count, rows, width), BF),
            jax.ShapeDtypeStruct((slot_count, width), BF),
        ],
        in_specs=[pl.BlockSpec(memory_space=pltpu.SMEM)] * 2 + [whole] * 14,
        out_specs=[whole, whole],
        scratch_shapes=[
            pltpu.VMEM((count, rows, width), F32),
            pltpu.VMEM((count, rows, width), F32),
            pltpu.VMEM((count, rows, width), BF),
        ],
        compiler_params=pltpu.CompilerParams(vmem_limit_bytes=40 * 2**20),
        cost_estimate=pl.CostEstimate(
            flops=2 * count * rows * 6144 * width, bytes_accessed=10 * 2**20, transcendentals=0
        ),
    )(place_a, place_b, *first, *second, weight, resid, gain, targets)


def gate_up_kernel(
    order, a0, a1, a2, a3, a4, b0, b1, b2, b3, b4, gate, up, inverse_gain,
    out, gate_sum, up_sum, square_sum,
):
    half, step = pl.program_id(0), pl.program_id(1)
    last = pl.num_programs(1) - 1

    @pl.when(step == 0)
    def _():
        gate_sum[...] = jnp.zeros_like(gate_sum)
        up_sum[...] = jnp.zeros_like(up_sum)
        square_sum[...] = jnp.zeros_like(square_sum)

    def use(ref):
        block = ref[0]
        gate_sum[...] += jnp.dot(block, gate[0], preferred_element_type=F32)
        up_sum[...] += jnp.dot(block, up[0], preferred_element_type=F32)
        plain = block.astype(F32) * inverse_gain[0]
        squares = plain * plain
        lanes = square_sum.shape[1]
        total = square_sum[...]
        for at in range(0, squares.shape[1], lanes):
            total = total + squares[:, at : at + lanes]
        square_sum[...] = total

    bounds = (0, 4, 8, 12, 14, 16)
    for which, refs in enumerate(((a0, a1, a2, a3, a4), (b0, b1, b2, b3, b4))):
        for low, high, ref in zip(bounds[:-1], bounds[1:], refs):
            @pl.when((half == which) & (step >= low) & (step < high))
            def _(ref=ref):
                use(ref)

    @pl.when(step == last)
    def _():
        features = 6144
        mean_square = jnp.sum(square_sum[...], axis=1, keepdims=True) / features
        factor = lax.rsqrt(mean_square + 1e-05)
        gate_act = gate_sum[...] * factor
        up_act = up_sum[...] * factor
        out[...] = (gate_act * jax.nn.sigmoid(gate_act) * up_act).astype(BF)


def gate_up(order, first, second, gate, up, inverse_gain):
    rows, width = first[0].shape[1], first[0].shape[2]
    hidden = gate.shape[2]
    bounds = (0, 4, 8, 12, 14, 16)
    specs = []
    for which in range(2):
        for low, high in zip(bounds[:-1], bounds[1:]):
            def at(half, step, order, which=which, low=low, high=high):
                here = jnp.clip(step - low, 0, high - low - 1)
                other = 0 if which == 1 else high - low - 1
                return (jnp.where(half == which, here, other), 0, 0)

            specs.append(pl.BlockSpec((1, rows, width), at))

    def weight_at(half, step, order):
        return (order[half * 16 + step], 0, 0)

    return pl.pallas_call(
        gate_up_kernel,
        out_shape=jax.ShapeDtypeStruct((2 * rows, hidden), BF),
        grid_spec=pltpu.PrefetchScalarGridSpec(
            num_scalar_prefetch=1,
            grid=(2, 16),
            in_specs=specs
            + [
                pl.BlockSpec((1, width, hidden), weight_at),
                pl.BlockSpec((1, width, hidden), weight_at),
                pl.BlockSpec((1, 1, width), weight_at),
            ],
            out_specs=pl.BlockSpec((rows, hidden), lambda half, step, order: (half, 0)),
            scratch_shapes=[
                pltpu.VMEM((rows, hidden), F32),
                pltpu.VMEM((rows, hidden), F32),
                pltpu.VMEM((rows, 128), F32),
            ],
        ),
        compiler_params=pltpu.CompilerParams(vmem_limit_bytes=40 * 2**20),
        cost_estimate=pl.CostEstimate(
            flops=2 * 2 * rows * 6144 * hidden * 2, bytes_accessed=36 * 2**20, transcendentals=0
        ),
    )(order, *first, *second, gate, up, inverse_gain)


def attend(queries, key_states, corrupted_value_state, clean_heads, patch_heads):
    scale = 1.0 / math.sqrt(HEAD_SIZE)
    length, query_width = queries.shape[1], queries.shape[2]
    local_heads = query_width // HEAD_SIZE
    query = queries.reshape(length, local_heads, HEAD_SIZE)
    key, value = key_states[0], corrupted_value_state[0]
    scores = jnp.einsum("ijd,td->jit", query, key, preferred_element_type=F32) * scale
    places = jnp.arange(length)
    causal = places[:, None] >= places[None, :]
    scores = jnp.where(causal[None], scores, -jnp.inf)
    highest = jnp.max(scores, axis=-1, keepdims=True)
    raised = jnp.exp(scores - highest)
    probs = (raised / jnp.sum(raised, axis=-1, keepdims=True)).astype(BF)
    attended = jnp.einsum("jit,td->ijd", probs, value, preferred_element_type=F32).astype(BF)
    head_ids = lax.axis_index("head") * local_heads + jnp.arange(local_heads)
    chosen = jnp.any(patch_heads[0][:, None] == head_ids[None, :], axis=0)
    merged = jnp.where(
        chosen[None, :, None], clean_heads.reshape(length, local_heads, HEAD_SIZE), attended
    )
    return merged.reshape(length, query_width)


def per_device(
    queries,
    key_states,
    corrupted_value_state,
    clean_heads,
    patch_heads,
    out_weight,
    residual,
    norm_gain,
    expert_ids,
    route_weights,
    gate_weight,
    up_weight,
    down_weight,
):
    heads, experts = lax.axis_size("head"), lax.axis_size("expert")
    e_index = lax.axis_index("expert")
    z_index, y_index = e_index // RING, e_index % RING
    tokens, width = residual.shape[1], residual.shape[2]
    top = expert_ids.shape[2]
    capacity = 3 * tokens * top // (2 * heads)
    columns = width // experts

    weight_all = lax.all_gather(out_weight, "head", axis=0)

    resid_blocks = residual[0].reshape(tokens, experts, columns).transpose(1, 0, 2)
    id_block = jnp.zeros((tokens, 128), BF).at[:, :top].set(expert_ids[0].astype(BF))
    payload = jnp.concatenate(
        [resid_blocks, jnp.broadcast_to(id_block[None], (experts, tokens, 128))], axis=2
    )
    payload = lax.all_to_all(payload, "expert", split_axis=0, concat_axis=0, tiled=True)
    all_ids = payload[:, :, columns : columns + top].astype(jnp.int32)

    def ranked(ids):
        pairs = ids.reshape(ids.shape[0], -1)
        onehot = (pairs[:, :, None] == jnp.arange(heads)[None, None, :]).astype(jnp.int32)
        earlier = jnp.tril(jnp.ones((pairs.shape[1], pairs.shape[1]), jnp.int32), -1)
        counts = jnp.sum(earlier[None, :, :, None] * onehot[:, None, :, :], axis=2)
        return jnp.sum(onehot * counts, axis=2).reshape(ids.shape)

    prompts = jnp.arange(experts)
    slot_of = (
        all_ids * (experts * capacity) + prompts[:, None, None] * capacity + ranked(all_ids)
    )
    targets = slot_of.reshape(-1, top).T

    near = jnp.array([0, 2, 3, 1])
    prompt_z, prompt_y = near[(prompts // RING - z_index) % RING], near[(prompts % RING - y_index) % RING]
    place_a, place_b = prompt_y * RING + prompt_z, prompt_z * RING + prompt_y

    merged = attend(queries, key_states, corrupted_value_state, clean_heads, patch_heads)
    merged = merged.reshape(heads, tokens, merged.shape[1])
    merged = lax.all_to_all(merged, "head", split_axis=0, concat_axis=0, tiled=True)
    first, second = gather_two(merged[: heads // 2], merged[heads // 2 :])
    own_gain = lax.dynamic_slice(norm_gain, (e_index * columns,), (columns,))[None]
    projected, slots = project(
        place_a, place_b, first, second, weight_all, payload, own_gain, targets,
        heads * experts * capacity,
    )
    own_projected = lax.all_to_all(projected, "expert", split_axis=0, concat_axis=0, tiled=True)

    slots = slots.reshape(heads, experts * capacity, columns)
    slots = lax.all_to_all(slots, "head", split_axis=0, concat_axis=0, tiled=True)
    half_rows = heads // 2 * experts * capacity
    slots = slots.reshape(2, half_rows, columns)
    first, second = gather_two(slots[0], slots[1])
    steps = jnp.array(NEAR_FIRST)
    order_a = ((z_index + steps[None, :]) % RING) * RING + (y_index + steps[:, None]) % RING
    order_b = ((z_index + steps[:, None]) % RING) * RING + (y_index + steps[None, :]) % RING
    order = jnp.concatenate([order_a.reshape(-1), order_b.reshape(-1)])
    hidden = gate_up(
        order,
        first,
        second,
        gate_weight[0].reshape(experts, columns, -1),
        up_weight[0].reshape(experts, columns, -1),
        (1.0 / norm_gain).reshape(experts, 1, columns),
    )

    far = jnp.array(FAR_FIRST)
    outer, inner = far[:, None, None, None], far[None, :, None, None]
    source = jnp.arange(heads // 2)[None, None, :, None]
    slot = jnp.arange(capacity)[None, None, None, :]

    def row_of(step_z, step_y, source):
        prompt = ((z_index + step_z) % RING) * RING + (y_index + step_y) % RING
        return (source * experts + prompt) * capacity + slot

    rows_a = row_of(inner, outer, source).reshape(RING, -1)
    rows_b = row_of(outer, inner, source + heads // 2).reshape(RING, -1)
    rows = jnp.stack([rows_a, rows_b], axis=1).reshape(-1)
    picks = (rows[:, None] == jnp.arange(rows.shape[0])[None, :]).astype(BF)
    ordered = jnp.dot(picks, hidden, preferred_element_type=F32).astype(BF)
    ordered = ordered.reshape(RING, -1, hidden.shape[1])
    sums = [
        jnp.dot(ordered[at], down_weight[0], preferred_element_type=F32).astype(BF)
        for at in range(RING)
    ]
    group = sums[0].shape[0] // 2
    total_a = ring_sum(*[part[:group] for part in sums], y_pairs, 0)
    total_b = ring_sum(*[part[group:] for part in sums], z_pairs, 0)
    total_a = total_a.reshape(RING, -1, width)
    total_b = total_b.reshape(RING, -1, width)
    total_a = ring_sum(*[total_a[at] for at in range(RING)], z_pairs, 1)
    total_b = ring_sum(*[total_b[at] for at in range(RING)], y_pairs, 1)
    totals = jnp.concatenate([total_a, total_b], axis=0).reshape(heads, capacity, width)
    returned = lax.all_to_all(totals, "head", split_axis=0, concat_axis=0, tiled=True)
    returned = returned.reshape(heads * capacity, width)

    own_slots = expert_ids[0] * capacity + ranked(expert_ids)[0]
    hidden_in = residual[0].astype(F32) + own_projected.transpose(1, 0, 2).reshape(
        tokens, width
    ).astype(F32)
    layer_out = hidden_in
    for k in range(top):
        pick = (own_slots[:, k : k + 1] == jnp.arange(heads * capacity)[None, :]).astype(BF)
        picked = jnp.dot(pick, returned, preferred_element_type=F32)
        layer_out = layer_out + picked * route_weights[0][:, k : k + 1]
    return layer_out.astype(BF).reshape(residual.shape)


def solution(mesh):
    placed = (
        P("expert", None, "head"),
        P("expert", None, "head"),
        P("expert", None, "head"),
        P("expert", None, "head"),
        P("expert", None),
        P("head", "expert"),
        P("expert", "head", None),
        P(),
        P("expert", "head", None),
        P("expert", "head", None),
        P("head", None, "expert"),
        P("head", None, "expert"),
        P("head", "expert", None),
    )
    return jax.shard_map(
        per_device, mesh=mesh, in_specs=placed, out_specs=P("expert", "head", None), check_vma=False
    )
```

```python
import math

import jax
import jax.numpy as jnp
from jax import lax
from jax.experimental import pallas as pl
from jax.experimental.pallas import tpu as pltpu
from jax.sharding import PartitionSpec as P

HEAD_SIZE = 128
RING = 4
NEAR_FIRST = (0, -1, 1, 2)
FAR_FIRST = (2, 1, -1, 0)
BF = jnp.bfloat16
F32 = jnp.float32


def ring_pairs(near, step):
    pairs = []
    for head in range(8):
        for z in range(RING):
            for y in range(RING):
                if near == (head % 2 == 0):
                    target = ((z + step) % RING) * RING + y
                else:
                    target = z * RING + (y + step) % RING
                pairs.append((head * 16 + z * RING + y, head * 16 + target))
    return pairs


def send(block, near, step):
    return lax.ppermute(block, ("head", "expert"), ring_pairs(near, step))


def gather_near(block):
    half = block.shape[0] // 2
    up = send(block, True, 1)
    down = send(block, True, -1)
    far_low = send(up[:half], True, 1)
    far_high = send(down[half:], True, -1)
    return jnp.stack([block, up, down, jnp.concatenate([far_low, far_high], axis=0)])


def gather_far(stack):
    half = RING // 2
    up = send(stack, False, 1)
    down = send(stack, False, -1)
    far_low = send(up[:half], False, 1)
    far_high = send(down[half:], False, -1)
    return up, down, far_low, far_high


def project_kernel(
    place, own, up, down, far_low, far_high, weight, resid, gain, targets,
    projected, slots, total, rows,
):
    count, width = projected.shape[0], projected.shape[2]
    acc = None
    for group in range(own.shape[1]):
        pieces = [ref[:, group] for ref in (own, up, down, far_low, far_high)]
        block = jnp.concatenate(pieces, axis=0)
        block = block.reshape(-1, block.shape[-1])
        term = jnp.dot(block, weight[group], preferred_element_type=F32)
        acc = term if acc is None else acc + term
    total[...] = acc.reshape(total.shape)
    for prompt in range(count):
        value = total[place[prompt]]
        projected[prompt] = value.astype(BF)
        hidden = value + resid[prompt][:, :width].astype(F32)
        rows[prompt] = (hidden * gain[...]).astype(BF)
    tokens = rows[...].reshape(-1, width)
    slot_ids = lax.broadcasted_iota(jnp.int32, (slots.shape[0], tokens.shape[0]), 0)
    chosen = (slot_ids == targets[0:1, :]) | (slot_ids == targets[1:2, :])
    dispatch = jnp.where(chosen, 1.0, 0.0).astype(BF)
    slots[...] = jnp.dot(dispatch, tokens, preferred_element_type=F32).astype(BF)


def project(place, blocks, weight, resid, gain, targets, slot_count):
    count, rows = resid.shape[0], resid.shape[1]
    width = weight.shape[2]
    whole = pl.BlockSpec(memory_space=pltpu.VMEM)
    return pl.pallas_call(
        project_kernel,
        out_shape=[
            jax.ShapeDtypeStruct((count, rows, width), BF),
            jax.ShapeDtypeStruct((slot_count, width), BF),
        ],
        in_specs=[pl.BlockSpec(memory_space=pltpu.SMEM)] + [whole] * 9,
        out_specs=[whole, whole],
        scratch_shapes=[
            pltpu.VMEM((count, rows, width), F32),
            pltpu.VMEM((count, rows, width), BF),
        ],
        compiler_params=pltpu.CompilerParams(vmem_limit_bytes=24 * 2**20),
        cost_estimate=pl.CostEstimate(
            flops=2 * count * rows * 6144 * width, bytes_accessed=10 * 2**20, transcendentals=0
        ),
    )(place, *blocks, weight, resid, gain, targets)


def gate_up_kernel(bounds, finish, begun, order, *refs):
    count = len(bounds) - 1
    blocks, refs = refs[:count], refs[count:]
    gate_low, gate_high, up_low, up_high, inverse_low, inverse_high = refs[:6]
    refs = refs[6:]
    if begun:
        gate_in, up_in, square_in = refs[:3]
        refs = refs[3:]
    if finish:
        row_of, out, gate_sum, up_sum, square_sum = refs
    else:
        gate_sum, up_sum, square_sum = refs
    step = pl.program_id(0)

    @pl.when(step == 0)
    def _():
        if begun:
            gate_sum[...] = gate_in[...]
            up_sum[...] = up_in[...]
            square_sum[...] = square_in[...]
        else:
            gate_sum[...] = jnp.zeros_like(gate_sum)
            up_sum[...] = jnp.zeros_like(up_sum)
            square_sum[...] = jnp.zeros_like(square_sum)

    def use(ref):
        block = jnp.concatenate([ref[0], ref[1]], axis=1)
        gate = jnp.concatenate([gate_low[0], gate_high[0]], axis=0)
        gate_sum[...] += jnp.dot(block, gate, preferred_element_type=F32)
        up = jnp.concatenate([up_low[0], up_high[0]], axis=0)
        up_sum[...] += jnp.dot(block, up, preferred_element_type=F32)
        lanes = square_sum.shape[1]
        total = square_sum[...]
        for at, inverse in ((0, inverse_low), (1, inverse_high)):
            plain = ref[at].astype(F32) * inverse[0]
            squares = plain * plain
            for lane in range(0, squares.shape[1], lanes):
                total = total + squares[:, lane : lane + lanes]
        square_sum[...] = total

    for low, high, ref in zip(bounds[:-1], bounds[1:], blocks):
        if count == 1:
            use(ref)
        else:
            @pl.when((step >= low) & (step < high))
            def _(ref=ref):
                use(ref)

    if finish:
        @pl.when(step == pl.num_programs(0) - 1)
        def _():
            features = 6144
            mean_square = jnp.sum(square_sum[...], axis=1, keepdims=True) / features
            factor = lax.rsqrt(mean_square + 1e-05)
            gate_act = gate_sum[...] * factor
            up_act = up_sum[...] * factor
            hidden = (gate_act * jax.nn.sigmoid(gate_act) * up_act).astype(BF)
            rows = hidden.shape[0]
            places = lax.broadcasted_iota(jnp.int32, (rows, rows), 1)
            picks = jnp.where(places == row_of[...], 1.0, 0.0).astype(BF)
            out[...] = jnp.dot(picks, hidden, preferred_element_type=F32).astype(BF)


def gate_up(order, blocks, gate, up, inverse_gain, sums=None, row_of=None):
    rows, width = blocks[0].shape[1], blocks[0].shape[2]
    hidden = gate.shape[2]
    bounds = [0]
    for block in blocks:
        bounds.append(bounds[-1] + block.shape[0] // 2)
    steps = bounds[-1]
    finish, begun = row_of is not None, sums is not None
    specs = []
    for low, high in zip(bounds[:-1], bounds[1:]):
        def at(step, order, low=low, high=high):
            return (jnp.clip(step - low, 0, high - low - 1), 0, 0)

        specs.append(pl.BlockSpec((2, rows, width), at))

    def low_at(step, order):
        return (order[2 * step], 0, 0)

    def high_at(step, order):
        return (order[2 * step + 1], 0, 0)

    for _ in range(2):
        specs += [pl.BlockSpec((1, width, hidden), low_at), pl.BlockSpec((1, width, hidden), high_at)]
    specs += [pl.BlockSpec((1, 1, width), low_at), pl.BlockSpec((1, 1, width), high_at)]
    sum_shapes = [(rows, hidden), (rows, hidden), (rows, 128)]
    operands = [*blocks, gate, gate, up, up, inverse_gain, inverse_gain]

    def whole(step, order):
        return (0, 0)

    if begun:
        specs += [pl.BlockSpec(shape, whole) for shape in sum_shapes]
        operands += list(sums)
    if finish:
        specs.append(pl.BlockSpec((rows, 1), whole))
        operands.append(row_of)
        out_shape = jax.ShapeDtypeStruct((rows, hidden), BF)
        out_specs = pl.BlockSpec((rows, hidden), whole)
        scratch = [pltpu.VMEM(shape, F32) for shape in sum_shapes]
    else:
        out_shape = [jax.ShapeDtypeStruct(shape, F32) for shape in sum_shapes]
        out_specs = [pl.BlockSpec(shape, whole) for shape in sum_shapes]
        scratch = []
    return pl.pallas_call(
        lambda *refs: gate_up_kernel(tuple(bounds), finish, begun, *refs),
        out_shape=out_shape,
        grid_spec=pltpu.PrefetchScalarGridSpec(
            num_scalar_prefetch=1,
            grid=(steps,),
            in_specs=specs,
            out_specs=out_specs,
            scratch_shapes=scratch,
        ),
        compiler_params=pltpu.CompilerParams(vmem_limit_bytes=36 * 2**20),
        cost_estimate=pl.CostEstimate(
            flops=8 * steps * rows * width * hidden,
            bytes_accessed=steps * 3 * 2**20,
            transcendentals=0,
        ),
    )(order, *operands)


def down_kernel(kind, hidden, weight, *refs):
    value = jnp.dot(hidden[0], weight[...], preferred_element_type=F32)
    half = value.shape[0] // 2
    if kind == "far":
        low, high = refs
        low[...] = value[:half].astype(BF)
        high[...] = value[half:].astype(BF)
    elif kind == "plus":
        came, out = refs
        out[:half] = (value[:half] + came[...].astype(F32)).astype(BF)
        out[half:] = value[half:].astype(BF)
    elif kind == "minus":
        came, out = refs
        out[:half] = value[:half].astype(BF)
        out[half:] = (value[half:] + came[...].astype(F32)).astype(BF)
    else:
        above, below, out = refs
        out[...] = (value + above[...].astype(F32) + below[...].astype(F32)).astype(BF)


def down(kind, at, hidden, weight, *came):
    rows, width = hidden.shape[1], weight.shape[1]
    step = 768
    parts = [(rows // 2,) * 2, (rows,)][kind != "far"]
    out_shape = [jax.ShapeDtypeStruct((part, width), BF) for part in parts]
    return pl.pallas_call(
        lambda *refs: down_kernel(kind, *refs),
        out_shape=out_shape,
        grid=(width // step,),
        in_specs=[
            pl.BlockSpec((1, rows, hidden.shape[2]), lambda n: (at, 0, 0)),
            pl.BlockSpec((weight.shape[0], step), lambda n: (0, n)),
        ]
        + [pl.BlockSpec((block.shape[0], step), lambda n: (0, n)) for block in came],
        out_specs=[pl.BlockSpec((part, step), lambda n: (0, n)) for part in parts],
        compiler_params=pltpu.CompilerParams(vmem_limit_bytes=16 * 2**20),
        cost_estimate=pl.CostEstimate(
            flops=2 * rows * hidden.shape[2] * width,
            bytes_accessed=8 * 2**20,
            transcendentals=0,
        ),
    )(hidden, weight, *came)


def ring_sum(blocks):
    half = blocks.shape[2] // 2
    from_minus = send(blocks[0, :, :half], True, 1)
    from_plus = send(blocks[0, :, half:], True, -1)
    plus, minus = blocks[1].astype(F32), blocks[2].astype(F32)
    plus = plus.at[:, :half].add(from_minus.astype(F32)).astype(BF)
    minus = minus.at[:, half:].add(from_plus.astype(F32)).astype(BF)
    above = send(plus, True, 1)
    below = send(minus, True, -1)
    return (blocks[3].astype(F32) + above.astype(F32) + below.astype(F32)).astype(BF)


def attend(queries, key_states, corrupted_value_state, clean_heads, patch_heads):
    scale = 1.0 / math.sqrt(HEAD_SIZE)
    length, query_width = queries.shape[1], queries.shape[2]
    local_heads = query_width // HEAD_SIZE
    query = queries.reshape(length, local_heads, HEAD_SIZE)
    key, value = key_states[0], corrupted_value_state[0]
    scores = jnp.einsum("ijd,td->jit", query, key, preferred_element_type=F32) * scale
    places = jnp.arange(length)
    causal = places[:, None] >= places[None, :]
    scores = jnp.where(causal[None], scores, -jnp.inf)
    highest = jnp.max(scores, axis=-1, keepdims=True)
    raised = jnp.exp(scores - highest)
    probs = (raised / jnp.sum(raised, axis=-1, keepdims=True)).astype(BF)
    attended = jnp.einsum("jit,td->ijd", probs, value, preferred_element_type=F32).astype(BF)
    head_ids = lax.axis_index("head") * local_heads + jnp.arange(local_heads)
    chosen = jnp.any(patch_heads[0][:, None] == head_ids[None, :], axis=0)
    merged = jnp.where(
        chosen[None, :, None], clean_heads.reshape(length, local_heads, HEAD_SIZE), attended
    )
    return merged.reshape(length, query_width)


def per_device(
    queries,
    key_states,
    corrupted_value_state,
    clean_heads,
    patch_heads,
    out_weight,
    residual,
    norm_gain,
    expert_ids,
    route_weights,
    gate_weight,
    up_weight,
    down_weight,
):
    heads, experts = lax.axis_size("head"), lax.axis_size("expert")
    e_index = lax.axis_index("expert")
    z_index, y_index = e_index // RING, e_index % RING
    first_core = lax.axis_index("head") % 2 == 0
    near_index, far_index = (
        jnp.where(first_core, z_index, y_index),
        jnp.where(first_core, y_index, z_index),
    )
    tokens, width = residual.shape[1], residual.shape[2]
    top = expert_ids.shape[2]
    capacity = 3 * tokens * top // (2 * heads)
    columns = width // experts

    def place_of(near, far):
        return jnp.where(first_core, near * RING + far, far * RING + near)

    weight_all = lax.all_gather(out_weight, "head", axis=0)
    merged = attend(queries, key_states, corrupted_value_state, clean_heads, patch_heads)
    merged = merged.reshape(heads, tokens, merged.shape[1])
    merged = lax.all_to_all(merged, "head", split_axis=0, concat_axis=0, tiled=True)
    stack = gather_near(merged)

    pairs = expert_ids.reshape(-1)
    onehot = (pairs[:, None] == jnp.arange(heads)[None, :]).astype(F32)
    earlier = (jnp.arange(pairs.shape[0])[:, None] > jnp.arange(pairs.shape[0])[None, :]).astype(F32)
    ranks = jnp.sum(onehot * jnp.dot(earlier, onehot), axis=1).astype(jnp.int32)
    ranks = ranks.reshape(tokens, top)

    resid_blocks = residual[0].reshape(tokens, experts, columns).transpose(1, 0, 2)
    id_block = jnp.concatenate([expert_ids[0], ranks], axis=1).astype(BF)
    id_block = jnp.pad(id_block, ((0, 0), (0, 128 - 2 * top)))
    payload = jnp.concatenate(
        [resid_blocks, jnp.broadcast_to(id_block[None], (experts, tokens, 128))], axis=2
    )
    payload = lax.all_to_all(payload, "expert", split_axis=0, concat_axis=0, tiled=True)
    marks = payload[:, :, columns : columns + 2 * top].astype(jnp.int32)
    prompts = jnp.arange(experts)
    targets = (marks[..., :top] * experts + prompts[:, None, None]) * capacity + marks[..., top:]
    targets = targets.reshape(-1, top).T

    nearness = jnp.array([0, 2, 3, 1])
    prompt_z, prompt_y = prompts // RING, prompts % RING
    prompt_near = jnp.where(first_core, prompt_z, prompt_y)
    prompt_far = jnp.where(first_core, prompt_y, prompt_z)
    place = nearness[(prompt_far - far_index) % RING] * RING + nearness[(prompt_near - near_index) % RING]

    own_gain = lax.dynamic_slice(norm_gain, (e_index * columns,), (columns,))[None]
    projected, slots = project(
        place, (stack, *gather_far(stack)), weight_all, payload, own_gain, targets,
        heads * experts * capacity,
    )
    own_projected = lax.all_to_all(projected, "expert", split_axis=0, concat_axis=0, tiled=True)

    slots = slots.reshape(heads, experts * capacity, columns)
    slots = lax.all_to_all(slots, "head", split_axis=0, concat_axis=0, tiled=True)
    stack = gather_near(slots.reshape(-1, columns))
    steps = jnp.array(NEAR_FIRST)
    order = place_of(
        (near_index + steps[None, :]) % RING, (far_index + steps[:, None]) % RING
    ).reshape(-1)
    gate = gate_weight[0].reshape(experts, columns, -1)
    up = up_weight[0].reshape(experts, columns, -1)
    inverse_gain = (1.0 / norm_gain).reshape(experts, 1, columns)
    above, below, far_low, far_high = gather_far(stack)
    sums = gate_up(order[:4], (stack,), gate, up, inverse_gain)
    sums = gate_up(order[4:12], (above, below), gate, up, inverse_gain, sums=sums)

    steps = jnp.array(FAR_FIRST)
    prompt = place_of(
        (near_index + steps[None, :]) % RING, (far_index + steps[:, None]) % RING
    )[:, :, None, None]
    source = jnp.arange(heads)[None, None, :, None]
    slot = jnp.arange(capacity)[None, None, None, :]
    row_of = ((source * experts + prompt) * capacity + slot).reshape(-1, 1)
    hidden = gate_up(
        order[12:], (far_low, far_high), gate, up, inverse_gain, sums=sums, row_of=row_of
    )
    hidden = hidden.reshape(RING, -1, hidden.shape[1])
    weight = down_weight[0]
    low, high = down("far", 0, hidden, weight)
    from_minus = send(low, False, 1)
    from_plus = send(high, False, -1)
    (plus,) = down("plus", 1, hidden, weight, from_minus)
    above = send(plus, False, 1)
    (minus,) = down("minus", 2, hidden, weight, from_plus)
    below = send(minus, False, -1)
    (total,) = down("own", 3, hidden, weight, above, below)
    totals = ring_sum(total.reshape(RING, -1, width)).reshape(heads, capacity, width)
    returned = lax.all_to_all(totals, "head", split_axis=0, concat_axis=0, tiled=True)
    returned = returned.reshape(heads * capacity, width)

    own_slots = expert_ids[0] * capacity + ranks
    hidden_in = residual[0].astype(F32) + own_projected.transpose(1, 0, 2).reshape(
        tokens, width
    ).astype(F32)
    layer_out = hidden_in
    for k in range(top):
        pick = (own_slots[:, k : k + 1] == jnp.arange(heads * capacity)[None, :]).astype(BF)
        picked = jnp.dot(pick, returned, preferred_element_type=F32)
        layer_out = layer_out + picked * route_weights[0][:, k : k + 1]
    return layer_out.astype(BF).reshape(residual.shape)


def solution(mesh):
    placed = (
        P("expert", None, "head"),
        P("expert", None, "head"),
        P("expert", None, "head"),
        P("expert", None, "head"),
        P("expert", None),
        P("head", "expert"),
        P("expert", "head", None),
        P(),
        P("expert", "head", None),
        P("expert", "head", None),
        P("head", None, "expert"),
        P("head", None, "expert"),
        P("head", "expert", None),
    )
    return jax.shard_map(
        per_device, mesh=mesh, in_specs=placed, out_specs=P("expert", "head", None), check_vma=False
    )
```

```python
import math

import jax
import jax.numpy as jnp
from jax import lax
from jax.experimental import pallas as pl
from jax.experimental.pallas import tpu as pltpu
from jax.sharding import PartitionSpec as P

HEAD_SIZE = 128
RING = 4
NEAR_FIRST = (0, -1, 1, 2)
FAR_FIRST = (2, 1, -1, 0)
BF = jnp.bfloat16
F32 = jnp.float32


def ring_pairs(near, step):
    pairs = []
    for head in range(8):
        for z in range(RING):
            for y in range(RING):
                if near == (head % 2 == 0):
                    target = ((z + step) % RING) * RING + y
                else:
                    target = z * RING + (y + step) % RING
                pairs.append((head * 16 + z * RING + y, head * 16 + target))
    return pairs


def send(block, near, step):
    return lax.ppermute(block, ("head", "expert"), ring_pairs(near, step))


def gather_pieces(block, after=None):
    half = block.shape[0] // 2
    up = send(block, True, 1)
    down = send(block, True, -1)
    first = jnp.stack([block, up])
    far_low = send(up[:half], True, 1)
    far_high = send(down[half:], True, -1)
    first_up = send(first, False, 1)
    first_down = send(first, False, -1)
    if after is not None:
        far_low, far_high, after = lax.optimization_barrier((far_low, far_high, after))
    second = jnp.stack([down, jnp.concatenate([far_low, far_high], axis=0)])
    second_up = send(second, False, 1)
    second_down = send(second, False, -1)
    return (first, second, first_up, first_down, second_up, second_down), after


def forward(first_up, second_down):
    return send(first_up, False, 1), send(second_down, False, -1)


PIECE_NEAR = ((0, -1), (1, 2), (0, -1), (0, -1), (1, 2), (1, 2), (0, -1), (1, 2))
PIECE_FAR = (0, 0, -1, 1, -1, 1, 2, 2)


def project_kernel(place, *refs):
    blocks, refs = refs[:8], refs[8:]
    weight, resid, gain, targets, projected, slots, held, total, rows, sems = refs
    count, width = projected.shape[0], projected.shape[2]
    groups = weight.shape[0]
    copies = [
        pltpu.make_async_copy(weight.at[group], held.at[group], sems.at[group])
        for group in range(groups)
    ]
    for copy in copies:
        copy.start()
    acc = None
    for group in range(groups):
        block = jnp.concatenate([ref[:, group] for ref in blocks], axis=0)
        block = block.reshape(-1, block.shape[-1])
        copies[group].wait()
        term = jnp.dot(block, held[group], preferred_element_type=F32)
        acc = term if acc is None else acc + term
    total[...] = acc.reshape(total.shape)
    for prompt in range(count):
        value = total[place[prompt]]
        projected[prompt] = value.astype(BF)
        hidden = value + resid[prompt][:, :width].astype(F32)
        rows[prompt] = (hidden * gain[...]).astype(BF)
    tokens = rows[...].reshape(-1, width)
    slot_ids = lax.broadcasted_iota(jnp.int32, (slots.shape[0], tokens.shape[0]), 0)
    chosen = (slot_ids == targets[0:1, :]) | (slot_ids == targets[1:2, :])
    dispatch = jnp.where(chosen, 1.0, 0.0).astype(BF)
    slots[...] = jnp.dot(dispatch, tokens, preferred_element_type=F32).astype(BF)


def project(place, blocks, weight, resid, gain, targets, slot_count):
    count, rows = resid.shape[0], resid.shape[1]
    groups, depth, width = weight.shape
    whole = pl.BlockSpec(memory_space=pltpu.VMEM)
    return pl.pallas_call(
        project_kernel,
        out_shape=[
            jax.ShapeDtypeStruct((count, rows, width), BF),
            jax.ShapeDtypeStruct((slot_count, width), BF),
        ],
        in_specs=[pl.BlockSpec(memory_space=pltpu.SMEM)]
        + [whole] * len(blocks)
        + [pl.BlockSpec(memory_space=pl.ANY)]
        + [whole] * 3,
        out_specs=[whole, whole],
        scratch_shapes=[
            pltpu.VMEM((groups, depth, width), BF),
            pltpu.VMEM((count, rows, width), F32),
            pltpu.VMEM((count, rows, width), BF),
            pltpu.SemaphoreType.DMA((groups,)),
        ],
        compiler_params=pltpu.CompilerParams(vmem_limit_bytes=56 * 2**20),
        cost_estimate=pl.CostEstimate(
            flops=2 * count * rows * 6144 * width, bytes_accessed=10 * 2**20, transcendentals=0
        ),
    )(place, *blocks, weight, resid, gain, targets)


def gate_up_kernel(bounds, finish, begun, order, *refs):
    count = len(bounds) - 1
    blocks, refs = refs[:count], refs[count:]
    gate_low, gate_high, up_low, up_high, inverse_low, inverse_high = refs[:6]
    refs = refs[6:]
    if begun:
        gate_in, up_in, square_in = refs[:3]
        refs = refs[3:]
    if finish:
        row_of, out, gate_sum, up_sum, square_sum = refs
    else:
        gate_sum, up_sum, square_sum = refs
    step = pl.program_id(0)

    @pl.when(step == 0)
    def _():
        if begun:
            gate_sum[...] = gate_in[...]
            up_sum[...] = up_in[...]
            square_sum[...] = square_in[...]
        else:
            gate_sum[...] = jnp.zeros_like(gate_sum)
            up_sum[...] = jnp.zeros_like(up_sum)
            square_sum[...] = jnp.zeros_like(square_sum)

    def use(ref):
        block = jnp.concatenate([ref[0], ref[1]], axis=1)
        gate = jnp.concatenate([gate_low[0], gate_high[0]], axis=0)
        gate_sum[...] += jnp.dot(block, gate, preferred_element_type=F32)
        up = jnp.concatenate([up_low[0], up_high[0]], axis=0)
        up_sum[...] += jnp.dot(block, up, preferred_element_type=F32)
        lanes = square_sum.shape[1]
        total = square_sum[...]
        for at, inverse in ((0, inverse_low), (1, inverse_high)):
            plain = ref[at].astype(F32) * inverse[0]
            squares = plain * plain
            for lane in range(0, squares.shape[1], lanes):
                total = total + squares[:, lane : lane + lanes]
        square_sum[...] = total

    for low, high, ref in zip(bounds[:-1], bounds[1:], blocks):
        if count == 1:
            use(ref)
        else:
            @pl.when((step >= low) & (step < high))
            def _(ref=ref):
                use(ref)

    if finish:
        @pl.when(step == pl.num_programs(0) - 1)
        def _():
            features = 6144
            mean_square = jnp.sum(square_sum[...], axis=1, keepdims=True) / features
            factor = lax.rsqrt(mean_square + 1e-05)
            gate_act = gate_sum[...] * factor
            up_act = up_sum[...] * factor
            hidden = (gate_act * jax.nn.sigmoid(gate_act) * up_act).astype(BF)
            rows = hidden.shape[0]
            places = lax.broadcasted_iota(jnp.int32, (rows, rows), 1)
            picks = jnp.where(places == row_of[...], 1.0, 0.0).astype(BF)
            out[...] = jnp.dot(picks, hidden, preferred_element_type=F32).astype(BF)


def gate_up(order, blocks, gate, up, inverse_gain, sums=None, row_of=None):
    rows, width = blocks[0].shape[1], blocks[0].shape[2]
    hidden = gate.shape[2]
    bounds = [0]
    for block in blocks:
        bounds.append(bounds[-1] + block.shape[0] // 2)
    steps = bounds[-1]
    finish, begun = row_of is not None, sums is not None
    specs = []
    for low, high in zip(bounds[:-1], bounds[1:]):
        def at(step, order, low=low, high=high):
            return (jnp.clip(step - low, 0, high - low - 1), 0, 0)

        specs.append(pl.BlockSpec((2, rows, width), at))

    def low_at(step, order):
        return (order[2 * step], 0, 0)

    def high_at(step, order):
        return (order[2 * step + 1], 0, 0)

    for _ in range(2):
        specs += [pl.BlockSpec((1, width, hidden), low_at), pl.BlockSpec((1, width, hidden), high_at)]
    specs += [pl.BlockSpec((1, 1, width), low_at), pl.BlockSpec((1, 1, width), high_at)]
    sum_shapes = [(rows, hidden), (rows, hidden), (rows, 128)]
    operands = [*blocks, gate, gate, up, up, inverse_gain, inverse_gain]

    def whole(step, order):
        return (0, 0)

    if begun:
        specs += [pl.BlockSpec(shape, whole) for shape in sum_shapes]
        operands += list(sums)
    if finish:
        specs.append(pl.BlockSpec((rows, 1), whole))
        operands.append(row_of)
        out_shape = jax.ShapeDtypeStruct((rows, hidden), BF)
        out_specs = pl.BlockSpec((rows, hidden), whole)
        scratch = [pltpu.VMEM(shape, F32) for shape in sum_shapes]
    else:
        out_shape = [jax.ShapeDtypeStruct(shape, F32) for shape in sum_shapes]
        out_specs = [pl.BlockSpec(shape, whole) for shape in sum_shapes]
        scratch = []
    return pl.pallas_call(
        lambda *refs: gate_up_kernel(tuple(bounds), finish, begun, *refs),
        out_shape=out_shape,
        grid_spec=pltpu.PrefetchScalarGridSpec(
            num_scalar_prefetch=1,
            grid=(steps,),
            in_specs=specs,
            out_specs=out_specs,
            scratch_shapes=scratch,
        ),
        compiler_params=pltpu.CompilerParams(vmem_limit_bytes=56 * 2**20),
        cost_estimate=pl.CostEstimate(
            flops=8 * steps * rows * width * hidden,
            bytes_accessed=steps * 3 * 2**20,
            transcendentals=0,
        ),
    )(order, *operands)


def down_kernel(hidden, weight, *outs):
    rows = hidden.shape[0] * hidden.shape[1]
    value = jnp.dot(
        hidden[...].reshape(rows, -1), weight[...], preferred_element_type=F32
    ).astype(BF)
    at = 0
    for out in outs:
        out[...] = value[at : at + out.shape[0]]
        at += out.shape[0]


def down(hidden, weight, piece, pieces, parts):
    groups, rows, depth = hidden.shape
    step = 768
    steps = weight.shape[1] // pieces // step
    return pl.pallas_call(
        down_kernel,
        out_shape=[jax.ShapeDtypeStruct((part, steps * step), BF) for part in parts],
        grid=(steps,),
        in_specs=[
            pl.BlockSpec((groups, rows, depth), lambda n: (0, 0, 0)),
            pl.BlockSpec((depth, step), lambda n: (0, piece * steps + n)),
        ],
        out_specs=[pl.BlockSpec((part, step), lambda n: (0, n)) for part in parts],
        compiler_params=pltpu.CompilerParams(vmem_limit_bytes=56 * 2**20),
        cost_estimate=pl.CostEstimate(
            flops=2 * groups * rows * depth * steps * step,
            bytes_accessed=8 * 2**20,
            transcendentals=0,
        ),
    )(hidden, weight)


def add(*terms):
    total = terms[0].astype(F32)
    for term in terms[1:]:
        total = total + term.astype(F32)
    return total.astype(BF)


def ring_sum(far_low, far_high, plus, minus, own, near, axis, after=None):
    half = far_low.shape[axis]
    low_came = send(far_low, near, 1)
    high_came = send(far_high, near, -1)
    low = lax.slice_in_dim(plus, 0, half, axis=axis)
    plus = lax.dynamic_update_slice_in_dim(plus, add(low, low_came), 0, axis)
    high = lax.slice_in_dim(minus, half, 2 * half, axis=axis)
    minus = lax.dynamic_update_slice_in_dim(minus, add(high, high_came), half, axis)
    above = send(plus, near, 1)
    below = send(minus, near, -1)
    if after is not None:
        above, below, after = lax.optimization_barrier((above, below, after))
    return add(own, above, below), after


def attend(queries, key_states, corrupted_value_state, clean_heads, patch_heads):
    scale = 1.0 / math.sqrt(HEAD_SIZE)
    length, query_width = queries.shape[1], queries.shape[2]
    local_heads = query_width // HEAD_SIZE
    query = queries.reshape(length, local_heads, HEAD_SIZE)
    key, value = key_states[0], corrupted_value_state[0]
    scores = jnp.einsum("ijd,td->jit", query, key, preferred_element_type=F32) * scale
    places = jnp.arange(length)
    causal = places[:, None] >= places[None, :]
    scores = jnp.where(causal[None], scores, -jnp.inf)
    highest = jnp.max(scores, axis=-1, keepdims=True)
    raised = jnp.exp(scores - highest)
    probs = (raised / jnp.sum(raised, axis=-1, keepdims=True)).astype(BF)
    attended = jnp.einsum("jit,td->ijd", probs, value, preferred_element_type=F32).astype(BF)
    head_ids = lax.axis_index("head") * local_heads + jnp.arange(local_heads)
    chosen = jnp.any(patch_heads[0][:, None] == head_ids[None, :], axis=0)
    merged = jnp.where(
        chosen[None, :, None], clean_heads.reshape(length, local_heads, HEAD_SIZE), attended
    )
    return merged.reshape(length, query_width)


def per_device(
    queries,
    key_states,
    corrupted_value_state,
    clean_heads,
    patch_heads,
    out_weight,
    residual,
    norm_gain,
    expert_ids,
    route_weights,
    gate_weight,
    up_weight,
    down_weight,
):
    heads, experts = lax.axis_size("head"), lax.axis_size("expert")
    e_index = lax.axis_index("expert")
    z_index, y_index = e_index // RING, e_index % RING
    first_core = lax.axis_index("head") % 2 == 0
    near_index, far_index = (
        jnp.where(first_core, z_index, y_index),
        jnp.where(first_core, y_index, z_index),
    )
    tokens, width = residual.shape[1], residual.shape[2]
    top = expert_ids.shape[2]
    capacity = 3 * tokens * top // (2 * heads)
    columns = width // experts

    def place_of(near, far):
        return jnp.where(first_core, near * RING + far, far * RING + near)

    weight_all = lax.all_gather(out_weight, "head", axis=0)
    merged = attend(queries, key_states, corrupted_value_state, clean_heads, patch_heads)
    merged = merged.reshape(heads, tokens, merged.shape[1])
    merged = lax.all_to_all(merged, "head", split_axis=0, concat_axis=0, tiled=True)
    pieces, _ = gather_pieces(merged)
    pieces = (*pieces, *forward(pieces[2], pieces[5]))

    pairs = expert_ids.reshape(-1)
    onehot = (pairs[:, None] == jnp.arange(heads)[None, :]).astype(F32)
    earlier = (jnp.arange(pairs.shape[0])[:, None] > jnp.arange(pairs.shape[0])[None, :]).astype(F32)
    ranks = jnp.sum(onehot * jnp.dot(earlier, onehot), axis=1).astype(jnp.int32)
    ranks = ranks.reshape(tokens, top)

    resid, _ = lax.optimization_barrier((residual[0], pieces[1]))
    resid_blocks = resid.reshape(tokens, experts, columns).transpose(1, 0, 2)
    id_block = jnp.concatenate([expert_ids[0], ranks], axis=1).astype(BF)
    id_block = jnp.pad(id_block, ((0, 0), (0, 128 - 2 * top)))
    payload = jnp.concatenate(
        [resid_blocks, jnp.broadcast_to(id_block[None], (experts, tokens, 128))], axis=2
    )
    payload = lax.all_to_all(payload, "expert", split_axis=0, concat_axis=0, tiled=True)
    marks = payload[:, :, columns : columns + 2 * top].astype(jnp.int32)
    prompts = jnp.arange(experts)
    targets = (marks[..., :top] * experts + prompts[:, None, None]) * capacity + marks[..., top:]
    targets = targets.reshape(-1, top).T

    near_steps = jnp.array(PIECE_NEAR)
    far_steps = jnp.array(PIECE_FAR)[:, None]
    order = place_of((near_index + near_steps) % RING, (far_index + far_steps) % RING).reshape(-1)
    at = jnp.arange(experts)
    place = jnp.sum(jnp.where(order[None, :] == at[:, None], at[None, :], 0), axis=1)

    own_gain = lax.dynamic_slice(norm_gain, (e_index * columns,), (columns,))[None]
    projected, slots = project(
        place, pieces, weight_all, payload, own_gain, targets,
        heads * experts * capacity,
    )
    own_projected = lax.all_to_all(projected, "expert", split_axis=0, concat_axis=0, tiled=True)

    slots = slots.reshape(heads, experts * capacity, columns)
    slots = lax.all_to_all(slots, "head", split_axis=0, concat_axis=0, tiled=True)
    pieces, own_projected = gather_pieces(slots.reshape(-1, columns), own_projected)
    first, second, first_up, first_down, second_up, second_down = pieces
    gate = gate_weight[0].reshape(experts, columns, -1)
    up = up_weight[0].reshape(experts, columns, -1)
    inverse_gain = (1.0 / norm_gain).reshape(experts, 1, columns)
    sums = gate_up(order[:8], (first, second, first_up, first_down), gate, up, inverse_gain)
    second_up, second_down, *sums = lax.optimization_barrier((second_up, second_down, *sums))
    far_first, far_second = forward(first_up, second_down)
    sums = gate_up(order[8:12], (second_up, second_down), gate, up, inverse_gain, sums=sums)

    steps = jnp.array(FAR_FIRST)
    prompt = place_of(
        (near_index + steps[None, :]) % RING, (far_index + steps[:, None]) % RING
    )[:, :, None, None]
    source = jnp.arange(heads)[None, None, :, None]
    slot = jnp.arange(capacity)[None, None, None, :]
    row_of = ((source * experts + prompt) * capacity + slot).reshape(-1, 1)
    hidden = gate_up(
        order[12:], (far_first, far_second), gate, up, inverse_gain, sums=sums, row_of=row_of
    )
    hidden = hidden.reshape(RING, -1, hidden.shape[1])
    weight = down_weight[0]
    rows = hidden.shape[1]
    own_slots = expert_ids[0] * capacity + ranks
    own_projected = own_projected.transpose(1, 0, 2).reshape(tokens, width)
    outputs = []
    pieces = 2
    wide = width // pieces
    totals = returned = None
    for piece in range(pieces):
        parts = down(hidden, weight, piece, pieces, (rows // 2, rows // 2, rows, rows, rows))
        total, _ = ring_sum(*parts, False, 0)
        if piece > 0:
            total, totals = lax.optimization_barrier((total, totals))
            returned = lax.all_to_all(totals, "head", split_axis=0, concat_axis=0, tiled=True)
        total = total.reshape(RING, -1, wide)
        totals, returned = ring_sum(
            total[0, :, : wide // 2], total[0, :, wide // 2 :], *total[1:], True, 1, returned
        )
        if piece > 0:
            outputs.append(returned)
        totals = totals.reshape(heads, capacity, wide)
    outputs.append(lax.all_to_all(totals, "head", split_axis=0, concat_axis=0, tiled=True))
    mixed = []
    for piece, returned in enumerate(outputs):
        returned = returned.reshape(heads * capacity, wide)
        at = slice(piece * wide, (piece + 1) * wide)
        layer_out = residual[0, :, at].astype(F32) + own_projected[:, at].astype(F32)
        for k in range(top):
            pick = (own_slots[:, k : k + 1] == jnp.arange(heads * capacity)[None, :]).astype(BF)
            picked = jnp.dot(pick, returned, preferred_element_type=F32)
            layer_out = layer_out + picked * route_weights[0][:, k : k + 1]
        mixed.append(layer_out.astype(BF))
    return jnp.concatenate(mixed, axis=1).reshape(residual.shape)


def solution(mesh):
    placed = (
        P("expert", None, "head"),
        P("expert", None, "head"),
        P("expert", None, "head"),
        P("expert", None, "head"),
        P("expert", None),
        P("head", "expert"),
        P("expert", "head", None),
        P(),
        P("expert", "head", None),
        P("expert", "head", None),
        P("head", None, "expert"),
        P("head", None, "expert"),
        P("head", "expert", None),
    )
    return jax.shard_map(
        per_device, mesh=mesh, in_specs=placed, out_specs=P("expert", "head", None), check_vma=False
    )
```

```python
import math

import jax
import jax.numpy as jnp
from jax import lax
from jax.experimental import pallas as pl
from jax.experimental.pallas import tpu as pltpu
from jax.sharding import PartitionSpec as P

HEAD_SIZE = 128
RING = 4
NEAR_FIRST = (0, -1, 1, 2)
FAR_FIRST = (2, 1, -1, 0)
BF = jnp.bfloat16
F32 = jnp.float32


def ring_pairs(near, step):
    pairs = []
    for head in range(8):
        for z in range(RING):
            for y in range(RING):
                if near == (head % 2 == 0):
                    target = ((z + step) % RING) * RING + y
                else:
                    target = z * RING + (y + step) % RING
                pairs.append((head * 16 + z * RING + y, head * 16 + target))
    return pairs


def send(block, near, step):
    return lax.ppermute(block, ("head", "expert"), ring_pairs(near, step))


def gather_pieces(block, after=None):
    half = block.shape[0] // 2
    up = send(block, True, 1)
    down = send(block, True, -1)
    first = jnp.stack([block, up])
    far_low = send(up[:half], True, 1)
    far_high = send(down[half:], True, -1)
    first_up = send(first, False, 1)
    first_down = send(first, False, -1)
    if after is not None:
        far_low, far_high, after = lax.optimization_barrier((far_low, far_high, after))
    second = jnp.stack([down, jnp.concatenate([far_low, far_high], axis=0)])
    second_up = send(second, False, 1)
    second_down = send(second, False, -1)
    return (first, second, first_up, first_down, second_up, second_down), after


def forward(first_up, second_down):
    return send(first_up, False, 1), send(second_down, False, -1)


PIECE_NEAR = ((0, -1), (1, 2), (0, -1), (0, -1), (1, 2), (1, 2), (0, -1), (1, 2))
PIECE_FAR = (0, 0, -1, 1, -1, 1, 2, 2)


def project_kernel(place, *refs):
    blocks, (weight, resid, gain, targets, projected, slots, total, rows) = refs[:8], refs[8:]
    count, width = projected.shape[0], projected.shape[2]
    acc = None
    for group in range(weight.shape[0]):
        block = jnp.concatenate([ref[:, group] for ref in blocks], axis=0)
        block = block.reshape(-1, block.shape[-1])
        term = jnp.dot(block, weight[group], preferred_element_type=F32)
        acc = term if acc is None else acc + term
    total[...] = acc.reshape(total.shape)
    for prompt in range(count):
        value = total[place[prompt]]
        projected[prompt] = value.astype(BF)
        hidden = value + resid[prompt][:, :width].astype(F32)
        rows[prompt] = (hidden * gain[...]).astype(BF)
    tokens = rows[...].reshape(-1, width)
    slot_ids = lax.broadcasted_iota(jnp.int32, (slots.shape[0], tokens.shape[0]), 0)
    chosen = (slot_ids == targets[0:1, :]) | (slot_ids == targets[1:2, :])
    dispatch = jnp.where(chosen, 1.0, 0.0).astype(BF)
    slots[...] = jnp.dot(dispatch, tokens, preferred_element_type=F32).astype(BF)


def project(place, blocks, weight, resid, gain, targets, slot_count):
    count, rows = resid.shape[0], resid.shape[1]
    width = weight.shape[2]
    whole = pl.BlockSpec(memory_space=pltpu.VMEM)
    return pl.pallas_call(
        project_kernel,
        out_shape=[
            jax.ShapeDtypeStruct((count, rows, width), BF),
            jax.ShapeDtypeStruct((slot_count, width), BF),
        ],
        in_specs=[pl.BlockSpec(memory_space=pltpu.SMEM)] + [whole] * (len(blocks) + 4),
        out_specs=[whole, whole],
        scratch_shapes=[
            pltpu.VMEM((count, rows, width), F32),
            pltpu.VMEM((count, rows, width), BF),
        ],
        compiler_params=pltpu.CompilerParams(vmem_limit_bytes=24 * 2**20),
        cost_estimate=pl.CostEstimate(
            flops=2 * count * rows * 6144 * width, bytes_accessed=10 * 2**20, transcendentals=0
        ),
    )(place, *blocks, weight, resid, gain, targets)


def gate_up_kernel(steps, finish, begun, order, *refs):
    count = sum(len(shapes) for shapes, _ in steps)
    blocks, refs = refs[:count], refs[count:]
    gate, up, inverse_gain = refs[:3]
    refs = refs[3:]
    if begun:
        gate_in, up_in, square_in = refs[:3]
        refs = refs[3:]
    if finish:
        row_of, out, gate_sum, up_sum, square_sum = refs[:5]
        refs = refs[5:]
    else:
        gate_sum, up_sum, square_sum = refs[:3]
        refs = refs[3:]
    held, weights, sems = refs[:count], refs[count : count + 2 * len(steps)], refs[-1]

    copies, at, place, sem = [], 0, 0, 0
    for step, (shapes, column) in enumerate(steps):
        mine = []
        for shape in shapes:
            mine.append(pltpu.make_async_copy(blocks[at], held[at], sems.at[sem]))
            at, sem = at + 1, sem + 1
        width = shapes[0][2]
        for index in range(sum(shape[0] for shape in shapes)):
            for source, target in ((gate, weights[2 * step]), (up, weights[2 * step + 1])):
                mine.append(
                    pltpu.make_async_copy(
                        source.at[order[place], pl.ds(column, width)],
                        target.at[pl.ds(index * width, width)],
                        sems.at[sem],
                    )
                )
                sem += 1
            place += 1
        copies.append(mine)
    for mine in copies:
        for copy in mine:
            copy.start()
    if begun:
        gate_sum[...] = gate_in[...]
        up_sum[...] = up_in[...]
    total = square_in[...] if begun else jnp.zeros(square_sum.shape, F32)
    lanes = square_sum.shape[1]
    at, place = 0, 0
    for step, (shapes, column) in enumerate(steps):
        for copy in copies[step]:
            copy.wait()
        pieces = []
        width = shapes[0][2]
        for shape in shapes:
            for index in range(shape[0]):
                pieces.append(held[at][index])
            at += 1
        block = jnp.concatenate(pieces, axis=1)
        gate_term = jnp.dot(block, weights[2 * step][...], preferred_element_type=F32)
        gate_sum[...] = gate_sum[...] + gate_term if begun or step > 0 else gate_term
        up_term = jnp.dot(block, weights[2 * step + 1][...], preferred_element_type=F32)
        up_sum[...] = up_sum[...] + up_term if begun or step > 0 else up_term
        for piece in pieces:
            inverse = inverse_gain[order[place]][:, column : column + width]
            plain = piece.astype(F32) * inverse
            squares = plain * plain
            for lane in range(0, width, lanes):
                total = total + squares[:, lane : lane + lanes]
            place += 1
    if not finish:
        square_sum[...] = total
    else:
        features = 6144
        mean_square = jnp.sum(total, axis=1, keepdims=True) / features
        factor = lax.rsqrt(mean_square + 1e-05)
        gate_act = gate_sum[...] * factor
        up_act = up_sum[...] * factor
        hidden = (gate_act * jax.nn.sigmoid(gate_act) * up_act).astype(BF)
        rows = hidden.shape[0]
        places = lax.broadcasted_iota(jnp.int32, (rows, rows), 1)
        picks = jnp.where(places == row_of[...], 1.0, 0.0).astype(BF)
        out[...] = jnp.dot(picks, hidden, preferred_element_type=F32).astype(BF)


def gate_up(order, steps, gate, up, inverse_gain, sums=None, row_of=None):
    blocks = [block for group, _ in steps for block in group]
    rows, hidden = blocks[0].shape[1], gate.shape[2]
    shapes = tuple((tuple(block.shape for block in group), column) for group, column in steps)
    finish, begun = row_of is not None, sums is not None
    any_place = pl.BlockSpec(memory_space=pl.ANY)
    whole = pl.BlockSpec(memory_space=pltpu.VMEM)
    sum_shapes = [(rows, hidden), (rows, hidden), (rows, 128)]
    operands = [order, *blocks, gate, up, inverse_gain]
    specs = [pl.BlockSpec(memory_space=pltpu.SMEM)] + [any_place] * (len(blocks) + 2) + [whole]
    if begun:
        operands += list(sums)
        specs += [whole] * 3
    scratch = []
    if finish:
        operands.append(row_of)
        specs.append(whole)
        out_shape = jax.ShapeDtypeStruct((rows, hidden), BF)
        out_specs = whole
        scratch += [pltpu.VMEM(shape, F32) for shape in sum_shapes]
    else:
        out_shape = [jax.ShapeDtypeStruct(shape, F32) for shape in sum_shapes]
        out_specs = [whole] * 3
    scratch += [pltpu.VMEM(block.shape, BF) for block in blocks]
    depth, copies = 0, len(blocks)
    for group, _ in steps:
        places = sum(block.shape[0] for block in group)
        scratch += [pltpu.VMEM((places * group[0].shape[2], hidden), BF)] * 2
        depth += places * group[0].shape[2]
        copies += 2 * places
    scratch.append(pltpu.SemaphoreType.DMA((copies,)))
    return pl.pallas_call(
        lambda *refs: gate_up_kernel(shapes, finish, begun, *refs),
        out_shape=out_shape,
        in_specs=specs,
        out_specs=out_specs,
        scratch_shapes=scratch,
        compiler_params=pltpu.CompilerParams(vmem_limit_bytes=48 * 2**20),
        cost_estimate=pl.CostEstimate(
            flops=4 * rows * depth * hidden,
            bytes_accessed=2 * depth * (rows + 2 * hidden),
            transcendentals=0,
        ),
    )(*operands)


def down_kernel(piece, hidden, weight, *refs):
    outs, held, sems = refs[:-2], refs[-2], refs[-1]
    rows = hidden.shape[0] * hidden.shape[1]
    chunks, _, step = held.shape
    copies = [
        pltpu.make_async_copy(
            weight.at[:, pl.ds((piece * chunks + chunk) * step, step)],
            held.at[chunk],
            sems.at[chunk],
        )
        for chunk in range(chunks)
    ]
    for copy in copies:
        copy.start()
    left = hidden[...].reshape(rows, -1)
    for chunk in range(chunks):
        copies[chunk].wait()
        value = jnp.dot(left, held[chunk], preferred_element_type=F32).astype(BF)
        at = 0
        for out in outs:
            out[:, chunk * step : (chunk + 1) * step] = value[at : at + out.shape[0]]
            at += out.shape[0]


def down(hidden, weight, piece, pieces, parts):
    groups, rows, depth = hidden.shape
    step = 768
    wide = weight.shape[1] // pieces
    whole = pl.BlockSpec(memory_space=pltpu.VMEM)
    return pl.pallas_call(
        lambda *refs: down_kernel(piece, *refs),
        out_shape=[jax.ShapeDtypeStruct((part, wide), BF) for part in parts],
        in_specs=[whole, pl.BlockSpec(memory_space=pl.ANY)],
        out_specs=[whole] * len(parts),
        scratch_shapes=[
            pltpu.VMEM((wide // step, depth, step), BF),
            pltpu.SemaphoreType.DMA((wide // step,)),
        ],
        compiler_params=pltpu.CompilerParams(vmem_limit_bytes=40 * 2**20),
        cost_estimate=pl.CostEstimate(
            flops=2 * groups * rows * depth * wide,
            bytes_accessed=8 * 2**20,
            transcendentals=0,
        ),
    )(hidden, weight)


def add(*terms):
    total = terms[0].astype(F32)
    for term in terms[1:]:
        total = total + term.astype(F32)
    return total.astype(BF)


def ring_sum(far_low, far_high, plus, minus, own, near, axis, after=None):
    half = far_low.shape[axis]
    low_came = send(far_low, near, 1)
    high_came = send(far_high, near, -1)
    low = lax.slice_in_dim(plus, 0, half, axis=axis)
    plus = lax.dynamic_update_slice_in_dim(plus, add(low, low_came), 0, axis)
    high = lax.slice_in_dim(minus, half, 2 * half, axis=axis)
    minus = lax.dynamic_update_slice_in_dim(minus, add(high, high_came), half, axis)
    above = send(plus, near, 1)
    below = send(minus, near, -1)
    if after is not None:
        above, below, after = lax.optimization_barrier((above, below, after))
    return add(own, above, below), after


def attend(queries, key_states, corrupted_value_state, clean_heads, patch_heads):
    scale = 1.0 / math.sqrt(HEAD_SIZE)
    length, query_width = queries.shape[1], queries.shape[2]
    local_heads = query_width // HEAD_SIZE
    query = queries.reshape(length, local_heads, HEAD_SIZE)
    key, value = key_states[0], corrupted_value_state[0]
    scores = jnp.einsum("ijd,td->jit", query, key, preferred_element_type=F32) * scale
    places = jnp.arange(length)
    causal = places[:, None] >= places[None, :]
    scores = jnp.where(causal[None], scores, -jnp.inf)
    highest = jnp.max(scores, axis=-1, keepdims=True)
    raised = jnp.exp(scores - highest)
    probs = (raised / jnp.sum(raised, axis=-1, keepdims=True)).astype(BF)
    attended = jnp.einsum("jit,td->ijd", probs, value, preferred_element_type=F32).astype(BF)
    head_ids = lax.axis_index("head") * local_heads + jnp.arange(local_heads)
    chosen = jnp.any(patch_heads[0][:, None] == head_ids[None, :], axis=0)
    merged = jnp.where(
        chosen[None, :, None], clean_heads.reshape(length, local_heads, HEAD_SIZE), attended
    )
    return merged.reshape(length, query_width)


def per_device(
    queries,
    key_states,
    corrupted_value_state,
    clean_heads,
    patch_heads,
    out_weight,
    residual,
    norm_gain,
    expert_ids,
    route_weights,
    gate_weight,
    up_weight,
    down_weight,
):
    heads, experts = lax.axis_size("head"), lax.axis_size("expert")
    e_index = lax.axis_index("expert")
    z_index, y_index = e_index // RING, e_index % RING
    first_core = lax.axis_index("head") % 2 == 0
    near_index, far_index = (
        jnp.where(first_core, z_index, y_index),
        jnp.where(first_core, y_index, z_index),
    )
    tokens, width = residual.shape[1], residual.shape[2]
    top = expert_ids.shape[2]
    capacity = 3 * tokens * top // (2 * heads)
    columns = width // experts

    def place_of(near, far):
        return jnp.where(first_core, near * RING + far, far * RING + near)

    weight_all = lax.all_gather(out_weight, "head", axis=0)
    merged = attend(queries, key_states, corrupted_value_state, clean_heads, patch_heads)
    merged = merged.reshape(heads, tokens, merged.shape[1])
    merged = lax.all_to_all(merged, "head", split_axis=0, concat_axis=0, tiled=True)
    pieces, _ = gather_pieces(merged)
    first_up, weight_all = lax.optimization_barrier((pieces[2], weight_all))
    pieces = (*pieces[:2], first_up, *pieces[3:])
    pieces = (*pieces, *forward(pieces[2], pieces[5]))

    pairs = expert_ids.reshape(-1)
    onehot = (pairs[:, None] == jnp.arange(heads)[None, :]).astype(F32)
    earlier = (jnp.arange(pairs.shape[0])[:, None] > jnp.arange(pairs.shape[0])[None, :]).astype(F32)
    ranks = jnp.sum(onehot * jnp.dot(earlier, onehot), axis=1).astype(jnp.int32)
    ranks = ranks.reshape(tokens, top)

    resid, _ = lax.optimization_barrier((residual[0], pieces[1]))
    resid_blocks = resid.reshape(tokens, experts, columns).transpose(1, 0, 2)
    id_block = jnp.concatenate([expert_ids[0], ranks], axis=1).astype(BF)
    id_block = jnp.pad(id_block, ((0, 0), (0, 128 - 2 * top)))
    payload = jnp.concatenate(
        [resid_blocks, jnp.broadcast_to(id_block[None], (experts, tokens, 128))], axis=2
    )
    payload = lax.all_to_all(payload, "expert", split_axis=0, concat_axis=0, tiled=True)
    marks = payload[:, :, columns : columns + 2 * top].astype(jnp.int32)
    prompts = jnp.arange(experts)
    targets = (marks[..., :top] * experts + prompts[:, None, None]) * capacity + marks[..., top:]
    targets = targets.reshape(-1, top).T

    near_steps = jnp.array(PIECE_NEAR)
    far_steps = jnp.array(PIECE_FAR)[:, None]
    order = place_of((near_index + near_steps) % RING, (far_index + far_steps) % RING).reshape(-1)
    at = jnp.arange(experts)
    place = jnp.sum(jnp.where(order[None, :] == at[:, None], at[None, :], 0), axis=1)

    own_gain = lax.dynamic_slice(norm_gain, (e_index * columns,), (columns,))[None]
    projected, slots = project(
        place, pieces, weight_all, payload, own_gain, targets,
        heads * experts * capacity,
    )
    own_projected = lax.all_to_all(projected, "expert", split_axis=0, concat_axis=0, tiled=True)

    slots = slots.reshape(heads, experts * capacity, columns)
    slots = lax.all_to_all(slots, "head", split_axis=0, concat_axis=0, tiled=True)
    pieces, own_projected = gather_pieces(slots.reshape(-1, columns), own_projected)
    first, second, first_up, first_down, second_up, second_down = pieces
    gate = gate_weight[0].reshape(experts, columns, -1)
    up = up_weight[0].reshape(experts, columns, -1)
    inverse_gain = (1.0 / norm_gain).reshape(experts, 1, columns)
    sums = gate_up(
        order[:8], [((block,), 0) for block in (first, second, first_up, first_down)],
        gate, up, inverse_gain,
    )
    second_up, second_down, *sums = lax.optimization_barrier((second_up, second_down, *sums))
    far_first, far_second = forward(first_up, second_down)
    sums = gate_up(
        order[8:12], [((second_up,), 0), ((second_down,), 0)], gate, up, inverse_gain, sums=sums
    )

    steps = jnp.array(FAR_FIRST)
    prompt = place_of(
        (near_index + steps[None, :]) % RING, (far_index + steps[:, None]) % RING
    )[:, :, None, None]
    source = jnp.arange(heads)[None, None, :, None]
    slot = jnp.arange(capacity)[None, None, None, :]
    row_of = ((source * experts + prompt) * capacity + slot).reshape(-1, 1)
    hidden = gate_up(
        order[12:], [((far_first,), 0), ((far_second,), 0)], gate, up, inverse_gain, sums=sums,
        row_of=row_of,
    )
    hidden = hidden.reshape(RING, -1, hidden.shape[1])
    weight = down_weight[0]
    rows = hidden.shape[1]
    own_slots = expert_ids[0] * capacity + ranks
    own_projected = own_projected.transpose(1, 0, 2).reshape(tokens, width)
    outputs = []
    pieces = 2
    wide = width // pieces
    totals = returned = None
    for piece in range(pieces):
        parts = down(hidden, weight, piece, pieces, (rows // 2, rows // 2, rows, rows, rows))
        total, _ = ring_sum(*parts, False, 0)
        if piece > 0:
            total, totals = lax.optimization_barrier((total, totals))
            returned = lax.all_to_all(totals, "head", split_axis=0, concat_axis=0, tiled=True)
        total = total.reshape(RING, -1, wide)
        totals, returned = ring_sum(
            total[0, :, : wide // 2], total[0, :, wide // 2 :], *total[1:], True, 1, returned
        )
        if piece > 0:
            outputs.append(returned)
        totals = totals.reshape(heads, capacity, wide)
    outputs.append(lax.all_to_all(totals, "head", split_axis=0, concat_axis=0, tiled=True))
    mixed = []
    for piece, returned in enumerate(outputs):
        returned = returned.reshape(heads * capacity, wide)
        at = slice(piece * wide, (piece + 1) * wide)
        layer_out = residual[0, :, at].astype(F32) + own_projected[:, at].astype(F32)
        for k in range(top):
            pick = (own_slots[:, k : k + 1] == jnp.arange(heads * capacity)[None, :]).astype(BF)
            picked = jnp.dot(pick, returned, preferred_element_type=F32)
            layer_out = layer_out + picked * route_weights[0][:, k : k + 1]
        mixed.append(layer_out.astype(BF))
    return jnp.concatenate(mixed, axis=1).reshape(residual.shape)


def solution(mesh):
    placed = (
        P("expert", None, "head"),
        P("expert", None, "head"),
        P("expert", None, "head"),
        P("expert", None, "head"),
        P("expert", None),
        P("head", "expert"),
        P("expert", "head", None),
        P(),
        P("expert", "head", None),
        P("expert", "head", None),
        P("head", None, "expert"),
        P("head", None, "expert"),
        P("head", "expert", None),
    )
    return jax.shard_map(
        per_device, mesh=mesh, in_specs=placed, out_specs=P("expert", "head", None), check_vma=False
    )
```

```python
import math

import jax
import jax.numpy as jnp
from jax import lax
from jax.experimental import pallas as pl
from jax.experimental.pallas import tpu as pltpu
from jax.sharding import PartitionSpec as P

HEAD_SIZE = 128
RING = 4
NEAR_FIRST = (0, -1, 1, 2)
FAR_FIRST = (2, 1, -1, 0)
BF = jnp.bfloat16
F32 = jnp.float32


def ring_pairs(near, step):
    pairs = []
    for head in range(8):
        for z in range(RING):
            for y in range(RING):
                if near == (head % 2 == 0):
                    target = ((z + step) % RING) * RING + y
                else:
                    target = z * RING + (y + step) % RING
                pairs.append((head * 16 + z * RING + y, head * 16 + target))
    return pairs


def send(block, near, step):
    return lax.ppermute(block, ("head", "expert"), ring_pairs(near, step))


def gather_pieces(block, direct=False):
    half = block.shape[0] // 2
    up = send(block, True, 1)
    down = send(block, True, -1)
    first = jnp.stack([block, up])
    if direct:
        far = send(block, True, 2)
    else:
        far_low = send(up[:half], True, 1)
        far_high = send(down[half:], True, -1)
        far = jnp.concatenate([far_low, far_high], axis=0)
    first_up = send(first, False, 1)
    first_down = send(first, False, -1)
    second = jnp.stack([down, far])
    second_up = send(second, False, 1)
    second_down = send(second, False, -1)
    return first, second, first_up, first_down, second_up, second_down


def forward(first_up, second_down):
    return send(first_up, False, 1), send(second_down, False, -1)


PIECE_NEAR = ((0, -1), (1, 2), (0, -1), (0, -1), (1, 2), (1, 2), (0, -1), (1, 2))
PIECE_FAR = (0, 0, -1, 1, -1, 1, 2, 2)


def in_hbm(array):
    return pltpu.with_memory_space_constraint(array, pltpu.HBM)


def project_kernel(place, *refs):
    blocks, (weight, resid, gain, targets, projected, slots, total, rows) = refs[:8], refs[8:]
    count, width = projected.shape[0], projected.shape[2]
    acc = None
    for group in range(weight.shape[0]):
        block = jnp.concatenate([ref[:, group] for ref in blocks], axis=0)
        block = block.reshape(-1, block.shape[-1])
        term = jnp.dot(block, weight[group], preferred_element_type=F32)
        acc = term if acc is None else acc + term
    total[...] = acc.reshape(total.shape)
    for prompt in range(count):
        value = total[place[prompt]]
        projected[prompt] = value.astype(BF)
        hidden = value + resid[prompt][:, :width].astype(F32)
        rows[prompt] = (hidden * gain[...]).astype(BF)
    tokens = rows[...].reshape(-1, width)
    slot_ids = lax.broadcasted_iota(jnp.int32, (slots.shape[0], tokens.shape[0]), 0)
    chosen = (slot_ids == targets[0:1, :]) | (slot_ids == targets[1:2, :])
    dispatch = jnp.where(chosen, 1.0, 0.0).astype(BF)
    slots[...] = jnp.dot(dispatch, tokens, preferred_element_type=F32).astype(BF)


def project(place, blocks, weight, resid, gain, targets, slot_count):
    count, rows = resid.shape[0], resid.shape[1]
    width = weight.shape[2]
    whole = pl.BlockSpec(memory_space=pltpu.VMEM)
    return pl.pallas_call(
        project_kernel,
        out_shape=[
            jax.ShapeDtypeStruct((count, rows, width), BF),
            jax.ShapeDtypeStruct((slot_count, width), BF),
        ],
        in_specs=[pl.BlockSpec(memory_space=pltpu.SMEM)] + [whole] * (len(blocks) + 4),
        out_specs=[whole, whole],
        scratch_shapes=[
            pltpu.VMEM((count, rows, width), F32),
            pltpu.VMEM((count, rows, width), BF),
        ],
        compiler_params=pltpu.CompilerParams(vmem_limit_bytes=24 * 2**20),
        cost_estimate=pl.CostEstimate(
            flops=2 * count * rows * 6144 * width, bytes_accessed=10 * 2**20, transcendentals=0
        ),
    )(place, *blocks, weight, resid, gain, targets)


def gate_up_kernel(steps, finish, begun, order, *refs):
    count = sum(len(shapes) for shapes, _ in steps)
    blocks, refs = refs[:count], refs[count:]
    gate, up, inverse_gain = refs[:3]
    refs = refs[3:]
    before, refs = (refs[:3], refs[3:]) if begun else ((), refs)
    if finish:
        row_of, out, gate_sum, up_sum, square_sum = refs[:5]
        refs = refs[5:]
    else:
        gate_sum, up_sum, square_sum = refs[:3]
        refs = refs[3:]
    held, weights, sems = refs[:count], refs[count : count + 2 * len(steps)], refs[-1]
    carried = refs[count + 2 * len(steps) : -1]

    copies, at, place, sem = [], 0, 0, 0
    for step, (shapes, column) in enumerate(steps):
        mine = []
        for shape in shapes:
            mine.append(pltpu.make_async_copy(blocks[at], held[at], sems.at[sem]))
            at, sem = at + 1, sem + 1
        width = shapes[0][2]
        for index in range(sum(shape[0] for shape in shapes)):
            for source, target in ((gate, weights[2 * step]), (up, weights[2 * step + 1])):
                mine.append(
                    pltpu.make_async_copy(
                        source.at[order[place], pl.ds(column, width)],
                        target.at[pl.ds(index * width, width)],
                        sems.at[sem],
                    )
                )
                sem += 1
            place += 1
        copies.append(mine)
    last = []
    for source, target in zip(before, carried):
        last.append(pltpu.make_async_copy(source, target, sems.at[sem]))
        sem += 1
    for mine in [*copies, last]:
        for copy in mine:
            copy.start()
    total = jnp.zeros(square_sum.shape, F32)
    lanes = square_sum.shape[1]
    at, place = 0, 0
    for step, (shapes, column) in enumerate(steps):
        for copy in copies[step]:
            copy.wait()
        pieces = []
        width = shapes[0][2]
        for shape in shapes:
            for index in range(shape[0]):
                pieces.append(held[at][index])
            at += 1
        block = jnp.concatenate(pieces, axis=1)
        gate_term = jnp.dot(block, weights[2 * step][...], preferred_element_type=F32)
        gate_sum[...] = gate_sum[...] + gate_term if step > 0 else gate_term
        up_term = jnp.dot(block, weights[2 * step + 1][...], preferred_element_type=F32)
        up_sum[...] = up_sum[...] + up_term if step > 0 else up_term
        for piece in pieces:
            inverse = inverse_gain[order[place]][:, column : column + width]
            plain = piece.astype(F32) * inverse
            squares = plain * plain
            for lane in range(0, width, lanes):
                total = total + squares[:, lane : lane + lanes]
            place += 1
    if begun:
        for copy in last:
            copy.wait()
        gate_sum[...] = gate_sum[...] + carried[0][...]
        up_sum[...] = up_sum[...] + carried[1][...]
        total = total + carried[2][...]
    if not finish:
        square_sum[...] = total
    else:
        features = 6144
        mean_square = jnp.sum(total, axis=1, keepdims=True) / features
        factor = lax.rsqrt(mean_square + 1e-05)
        gate_act = gate_sum[...] * factor
        up_act = up_sum[...] * factor
        hidden = (gate_act * jax.nn.sigmoid(gate_act) * up_act).astype(BF)
        rows = hidden.shape[0]
        places = lax.broadcasted_iota(jnp.int32, (rows, rows), 1)
        picks = jnp.where(places == row_of[...], 1.0, 0.0).astype(BF)
        out[...] = jnp.dot(picks, hidden, preferred_element_type=F32).astype(BF)


def gate_up(order, steps, gate, up, inverse_gain, sums=None, row_of=None):
    blocks = [block for group, _ in steps for block in group]
    rows, hidden = blocks[0].shape[1], gate.shape[2]
    shapes = tuple((tuple(block.shape for block in group), column) for group, column in steps)
    finish, begun = row_of is not None, sums is not None
    any_place = pl.BlockSpec(memory_space=pl.ANY)
    whole = pl.BlockSpec(memory_space=pltpu.VMEM)
    sum_shapes = [(rows, hidden), (rows, hidden), (rows, 128)]
    operands = [order, *blocks, gate, up, inverse_gain]
    specs = [pl.BlockSpec(memory_space=pltpu.SMEM)] + [any_place] * (len(blocks) + 2) + [whole]
    if begun:
        operands += list(sums)
        specs += [any_place] * 3
    scratch = []
    if finish:
        operands.append(row_of)
        specs.append(whole)
        out_shape = jax.ShapeDtypeStruct((rows, hidden), BF)
        out_specs = whole
        scratch += [pltpu.VMEM(shape, F32) for shape in sum_shapes]
    else:
        out_shape = [jax.ShapeDtypeStruct(shape, F32) for shape in sum_shapes]
        out_specs = [whole] * 3
    scratch += [pltpu.VMEM(block.shape, BF) for block in blocks]
    depth, copies = 0, len(blocks)
    for group, _ in steps:
        places = sum(block.shape[0] for block in group)
        scratch += [pltpu.VMEM((places * group[0].shape[2], hidden), BF)] * 2
        depth += places * group[0].shape[2]
        copies += 2 * places
    if begun:
        scratch += [pltpu.VMEM(shape, F32) for shape in sum_shapes]
        copies += 3
    scratch.append(pltpu.SemaphoreType.DMA((copies,)))
    return pl.pallas_call(
        lambda *refs: gate_up_kernel(shapes, finish, begun, *refs),
        out_shape=out_shape,
        in_specs=specs,
        out_specs=out_specs,
        scratch_shapes=scratch,
        compiler_params=pltpu.CompilerParams(vmem_limit_bytes=48 * 2**20),
        cost_estimate=pl.CostEstimate(
            flops=4 * rows * depth * hidden,
            bytes_accessed=2 * depth * (rows + 2 * hidden),
            transcendentals=0,
        ),
    )(*operands)


def down_kernel(piece, count, hidden, weight, *refs):
    outs, (held, made, sems, out_sems) = refs[:count], refs[count:]
    rows = hidden.shape[0] * hidden.shape[1]
    chunks, _, step = held.shape
    copies = [
        pltpu.make_async_copy(
            weight.at[:, pl.ds((piece * chunks + chunk) * step, step)],
            held.at[chunk],
            sems.at[chunk],
        )
        for chunk in range(chunks)
    ]
    for copy in copies:
        copy.start()
    left = hidden[...].reshape(rows, -1)
    leaving = []
    for chunk in range(chunks):
        copies[chunk].wait()
        made[chunk] = jnp.dot(left, held[chunk], preferred_element_type=F32).astype(BF)
        at = 0
        for index, out in enumerate(outs):
            leaving.append(
                pltpu.make_async_copy(
                    made.at[chunk, pl.ds(at, out.shape[0])],
                    out.at[:, pl.ds(chunk * step, step)],
                    out_sems.at[chunk, index],
                )
            )
            leaving[-1].start()
            at += out.shape[0]
    for copy in leaving:
        copy.wait()


def down(hidden, weight, piece, pieces, parts):
    groups, rows, depth = hidden.shape
    step = 768
    wide = weight.shape[1] // pieces
    chunks = wide // step
    any_place = pl.BlockSpec(memory_space=pl.ANY)
    return pl.pallas_call(
        lambda *refs: down_kernel(piece, len(parts), *refs),
        out_shape=[pltpu.HBM((part, wide), BF) for part in parts],
        in_specs=[pl.BlockSpec(memory_space=pltpu.VMEM), any_place],
        out_specs=[any_place] * len(parts),
        scratch_shapes=[
            pltpu.VMEM((chunks, depth, step), BF),
            pltpu.VMEM((chunks, groups * rows, step), BF),
            pltpu.SemaphoreType.DMA((chunks,)),
            pltpu.SemaphoreType.DMA((chunks, len(parts))),
        ],
        compiler_params=pltpu.CompilerParams(vmem_limit_bytes=24 * 2**20),
        cost_estimate=pl.CostEstimate(
            flops=2 * groups * rows * depth * wide,
            bytes_accessed=8 * 2**20,
            transcendentals=0,
        ),
    )(hidden, weight)


def add(*terms):
    total = terms[0].astype(F32)
    for term in terms[1:]:
        total = total + term.astype(F32)
    return total.astype(BF)


def ring_sum(far_low, far_high, plus, minus, own, near, axis):
    half = far_low.shape[axis]
    low_came = send(far_low, near, 1)
    high_came = send(far_high, near, -1)
    low = lax.slice_in_dim(plus, 0, half, axis=axis)
    plus = lax.dynamic_update_slice_in_dim(plus, add(low, low_came), 0, axis)
    high = lax.slice_in_dim(minus, half, 2 * half, axis=axis)
    minus = lax.dynamic_update_slice_in_dim(minus, add(high, high_came), half, axis)
    above = send(plus, near, 1)
    below = send(minus, near, -1)
    return add(own, above, below)


def attend(queries, key_states, corrupted_value_state, clean_heads, patch_heads):
    scale = 1.0 / math.sqrt(HEAD_SIZE)
    length, query_width = queries.shape[1], queries.shape[2]
    local_heads = query_width // HEAD_SIZE
    query = queries.reshape(length, local_heads, HEAD_SIZE)
    key, value = key_states[0], corrupted_value_state[0]
    scores = jnp.einsum("ijd,td->jit", query, key, preferred_element_type=F32) * scale
    places = jnp.arange(length)
    causal = places[:, None] >= places[None, :]
    scores = jnp.where(causal[None], scores, -jnp.inf)
    highest = jnp.max(scores, axis=-1, keepdims=True)
    raised = jnp.exp(scores - highest)
    probs = (raised / jnp.sum(raised, axis=-1, keepdims=True)).astype(BF)
    attended = jnp.einsum("jit,td->ijd", probs, value, preferred_element_type=F32).astype(BF)
    head_ids = lax.axis_index("head") * local_heads + jnp.arange(local_heads)
    chosen = jnp.any(patch_heads[0][:, None] == head_ids[None, :], axis=0)
    merged = jnp.where(
        chosen[None, :, None], clean_heads.reshape(length, local_heads, HEAD_SIZE), attended
    )
    return merged.reshape(length, query_width)


def per_device(
    queries,
    key_states,
    corrupted_value_state,
    clean_heads,
    patch_heads,
    out_weight,
    residual,
    norm_gain,
    expert_ids,
    route_weights,
    gate_weight,
    up_weight,
    down_weight,
):
    heads, experts = lax.axis_size("head"), lax.axis_size("expert")
    e_index = lax.axis_index("expert")
    z_index, y_index = e_index // RING, e_index % RING
    first_core = lax.axis_index("head") % 2 == 0
    near_index, far_index = (
        jnp.where(first_core, z_index, y_index),
        jnp.where(first_core, y_index, z_index),
    )
    tokens, width = residual.shape[1], residual.shape[2]
    top = expert_ids.shape[2]
    capacity = 3 * tokens * top // (2 * heads)
    columns = width // experts

    def place_of(near, far):
        return jnp.where(first_core, near * RING + far, far * RING + near)

    weight_all = lax.all_gather(out_weight, "head", axis=0)
    merged = attend(queries, key_states, corrupted_value_state, clean_heads, patch_heads)
    merged = merged.reshape(heads, tokens, merged.shape[1])
    merged = lax.all_to_all(merged, "head", split_axis=0, concat_axis=0, tiled=True)
    pieces = gather_pieces(merged, direct=True)
    first_up, weight_all = lax.optimization_barrier((pieces[2], weight_all))
    pieces = (*pieces[:2], first_up, *pieces[3:])
    pieces = (*pieces, *forward(pieces[2], pieces[5]))

    pairs = expert_ids.reshape(-1)
    onehot = (pairs[:, None] == jnp.arange(heads)[None, :]).astype(F32)
    earlier = (jnp.arange(pairs.shape[0])[:, None] > jnp.arange(pairs.shape[0])[None, :]).astype(F32)
    ranks = jnp.sum(onehot * jnp.dot(earlier, onehot), axis=1).astype(jnp.int32)
    ranks = ranks.reshape(tokens, top)

    resid, _ = lax.optimization_barrier((residual[0], pieces[1]))
    resid_blocks = resid.reshape(tokens, experts, columns).transpose(1, 0, 2)
    id_block = jnp.concatenate([expert_ids[0], ranks], axis=1).astype(BF)
    id_block = jnp.pad(id_block, ((0, 0), (0, 128 - 2 * top)))
    payload = jnp.concatenate(
        [resid_blocks, jnp.broadcast_to(id_block[None], (experts, tokens, 128))], axis=2
    )
    payload = lax.all_to_all(payload, "expert", split_axis=0, concat_axis=0, tiled=True)
    marks = payload[:, :, columns : columns + 2 * top].astype(jnp.int32)
    prompts = jnp.arange(experts)
    targets = (marks[..., :top] * experts + prompts[:, None, None]) * capacity + marks[..., top:]
    targets = targets.reshape(-1, top).T

    near_steps = jnp.array(PIECE_NEAR)
    far_steps = jnp.array(PIECE_FAR)[:, None]
    order = place_of((near_index + near_steps) % RING, (far_index + far_steps) % RING).reshape(-1)
    at = jnp.arange(experts)
    place = jnp.sum(jnp.where(order[None, :] == at[:, None], at[None, :], 0), axis=1)

    own_gain = lax.dynamic_slice(norm_gain, (e_index * columns,), (columns,))[None]
    projected, slots = project(
        place, pieces, weight_all, payload, own_gain, targets,
        heads * experts * capacity,
    )
    own_projected = lax.all_to_all(projected, "expert", split_axis=0, concat_axis=0, tiled=True)

    slots = slots.reshape(heads, experts * capacity, columns)
    slots = lax.all_to_all(slots, "head", split_axis=0, concat_axis=0, tiled=True)
    pieces = gather_pieces(slots.reshape(-1, columns))
    first, second, first_up, first_down, second_up, second_down = pieces
    gate = in_hbm(gate_weight[0].reshape(experts, columns, -1))
    up = in_hbm(up_weight[0].reshape(experts, columns, -1))
    inverse_gain = (1.0 / norm_gain).reshape(experts, 1, columns)
    sums = gate_up(
        order[:8], [((block,), 0) for block in (first, second, first_up, first_down)],
        gate, up, inverse_gain,
    )
    second_up, second_down, own_projected, *sums = lax.optimization_barrier(
        (second_up, second_down, own_projected, *sums)
    )
    far_first, far_second = forward(first_up, second_down)
    sums = gate_up(
        order[8:12], [((second_up,), 0), ((second_down,), 0)], gate, up, inverse_gain, sums=sums
    )

    steps = jnp.array(FAR_FIRST)
    prompt = place_of(
        (near_index + steps[None, :]) % RING, (far_index + steps[:, None]) % RING
    )[:, :, None, None]
    source = jnp.arange(heads)[None, None, :, None]
    slot = jnp.arange(capacity)[None, None, None, :]
    row_of = ((source * experts + prompt) * capacity + slot).reshape(-1, 1)
    hidden = gate_up(
        order[12:], [((far_first,), 0), ((far_second,), 0)], gate, up, inverse_gain, sums=sums,
        row_of=row_of,
    )
    hidden = hidden.reshape(RING, -1, hidden.shape[1])
    weight = in_hbm(down_weight[0])
    rows = hidden.shape[1]
    own_slots = expert_ids[0] * capacity + ranks
    own_projected = own_projected.transpose(1, 0, 2).reshape(tokens, width)
    outputs = []
    pieces = 2
    wide = width // pieces
    totals = returned = None
    for piece in range(pieces):
        parts = down(hidden, weight, piece, pieces, (rows // 2, rows // 2, rows, rows, rows))
        total = ring_sum(*parts, False, 0)
        if piece > 0:
            total, _ = lax.optimization_barrier((total, totals))
            returned = lax.all_to_all(totals, "head", split_axis=0, concat_axis=0, tiled=True)
        total = total.reshape(RING, -1, wide)
        came = [send(total[at], True, step) for at, step in enumerate(FAR_FIRST[:3])]
        if returned is not None:
            *came, returned = lax.optimization_barrier((*came, returned))
        totals = add(total[3], *came)
        if piece > 0:
            outputs.append(returned)
        totals = totals.reshape(heads, capacity, wide)
    outputs.append(lax.all_to_all(totals, "head", split_axis=0, concat_axis=0, tiled=True))
    mixed = []
    for piece, returned in enumerate(outputs):
        returned = returned.reshape(heads * capacity, wide)
        at = slice(piece * wide, (piece + 1) * wide)
        layer_out = residual[0, :, at].astype(F32) + own_projected[:, at].astype(F32)
        for k in range(top):
            pick = (own_slots[:, k : k + 1] == jnp.arange(heads * capacity)[None, :]).astype(BF)
            picked = jnp.dot(pick, returned, preferred_element_type=F32)
            layer_out = layer_out + picked * route_weights[0][:, k : k + 1]
        mixed.append(layer_out.astype(BF))
    return jnp.concatenate(mixed, axis=1).reshape(residual.shape)


def solution(mesh):
    placed = (
        P("expert", None, "head"),
        P("expert", None, "head"),
        P("expert", None, "head"),
        P("expert", None, "head"),
        P("expert", None),
        P("head", "expert"),
        P("expert", "head", None),
        P(),
        P("expert", "head", None),
        P("expert", "head", None),
        P("head", None, "expert"),
        P("head", None, "expert"),
        P("head", "expert", None),
    )
    return jax.shard_map(
        per_device, mesh=mesh, in_specs=placed, out_specs=P("expert", "head", None), check_vma=False
    )
```

```python
import math

import jax
import jax.numpy as jnp
from jax import lax
from jax.experimental import pallas as pl
from jax.experimental.pallas import tpu as pltpu
from jax.sharding import PartitionSpec as P

HEAD_SIZE = 128
RING = 4
NEAR_FIRST = (0, -1, 1, 2)
FAR_FIRST = (2, 1, -1, 0)
BF = jnp.bfloat16
F32 = jnp.float32


def ring_pairs(near, step):
    pairs = []
    for head in range(8):
        for z in range(RING):
            for y in range(RING):
                if near == (head % 2 == 0):
                    target = ((z + step) % RING) * RING + y
                else:
                    target = z * RING + (y + step) % RING
                pairs.append((head * 16 + z * RING + y, head * 16 + target))
    return pairs


def send(block, near, step):
    return lax.ppermute(block, ("head", "expert"), ring_pairs(near, step))


def gather_pieces(block, direct=False, after=None):
    half = block.shape[0] // 2
    up = send(block, True, 1)
    down = send(block, True, -1)
    first = jnp.stack([block, up])
    if direct:
        far = send(block, True, 2)
    else:
        far_low = send(up[:half], True, 1)
        far_high = send(down[half:], True, -1)
        if after is not None:
            far_low, far_high, after = lax.optimization_barrier((far_low, far_high, after))
        far = jnp.concatenate([far_low, far_high], axis=0)
    first_up = send(first, False, 1)
    first_down = send(first, False, -1)
    second = jnp.stack([down, far])
    second_up = send(second, False, 1)
    second_down = send(second, False, -1)
    return (first, second, first_up, first_down, second_up, second_down), after


def forward(first_up, second_down):
    return send(first_up, False, 1), send(second_down, False, -1)


PIECE_NEAR = ((0, -1), (1, 2), (0, -1), (0, -1), (1, 2), (1, 2), (0, -1), (1, 2))
PIECE_FAR = (0, 0, -1, 1, -1, 1, 2, 2)


def in_hbm(array):
    return pltpu.with_memory_space_constraint(array, pltpu.HBM)


def project_kernel(place, *refs):
    blocks, (weight, resid, gain, targets, projected, slots, total, rows) = refs[:8], refs[8:]
    count, width = projected.shape[0], projected.shape[2]
    acc = None
    for group in range(weight.shape[0]):
        block = jnp.concatenate([ref[:, group] for ref in blocks], axis=0)
        block = block.reshape(-1, block.shape[-1])
        term = jnp.dot(block, weight[group], preferred_element_type=F32)
        acc = term if acc is None else acc + term
    total[...] = acc.reshape(total.shape)
    for prompt in range(count):
        value = total[place[prompt]]
        projected[prompt] = value.astype(BF)
        hidden = value + resid[prompt][:, :width].astype(F32)
        rows[prompt] = (hidden * gain[...]).astype(BF)
    tokens = rows[...].reshape(-1, width)
    slot_ids = lax.broadcasted_iota(jnp.int32, (slots.shape[0], tokens.shape[0]), 0)
    chosen = (slot_ids == targets[0:1, :]) | (slot_ids == targets[1:2, :])
    dispatch = jnp.where(chosen, 1.0, 0.0).astype(BF)
    slots[...] = jnp.dot(dispatch, tokens, preferred_element_type=F32).astype(BF)


def project(place, blocks, weight, resid, gain, targets, slot_count):
    count, rows = resid.shape[0], resid.shape[1]
    width = weight.shape[2]
    whole = pl.BlockSpec(memory_space=pltpu.VMEM)
    return pl.pallas_call(
        project_kernel,
        out_shape=[
            jax.ShapeDtypeStruct((count, rows, width), BF),
            jax.ShapeDtypeStruct((slot_count, width), BF),
        ],
        in_specs=[pl.BlockSpec(memory_space=pltpu.SMEM)] + [whole] * (len(blocks) + 4),
        out_specs=[whole, whole],
        scratch_shapes=[
            pltpu.VMEM((count, rows, width), F32),
            pltpu.VMEM((count, rows, width), BF),
        ],
        compiler_params=pltpu.CompilerParams(vmem_limit_bytes=24 * 2**20),
        cost_estimate=pl.CostEstimate(
            flops=2 * count * rows * 6144 * width, bytes_accessed=10 * 2**20, transcendentals=0
        ),
    )(place, *blocks, weight, resid, gain, targets)


DOWN_STEP = 768


def down_scratch(rows, depth, wide, parts):
    chunks = wide // DOWN_STEP
    return [
        pltpu.VMEM((chunks, depth, DOWN_STEP), BF),
        pltpu.VMEM((chunks, rows, DOWN_STEP), BF),
        pltpu.SemaphoreType.DMA((chunks,)),
        pltpu.SemaphoreType.DMA((chunks, parts)),
    ]


def down_reads(weight, held, sems, start):
    return [
        pltpu.make_async_copy(
            weight.at[:, pl.ds(start + chunk * DOWN_STEP, DOWN_STEP)],
            held.at[chunk],
            sems.at[chunk],
        )
        for chunk in range(held.shape[0])
    ]


def down_products(left, copies, held, made, out_sems, outs):
    leaving = []
    for chunk, copy in enumerate(copies):
        copy.wait()
        made[chunk] = jnp.dot(left, held[chunk], preferred_element_type=F32).astype(BF)
        at = 0
        for index, out in enumerate(outs):
            leaving.append(
                pltpu.make_async_copy(
                    made.at[chunk, pl.ds(at, out.shape[0])],
                    out.at[:, pl.ds(chunk * DOWN_STEP, DOWN_STEP)],
                    out_sems.at[chunk, index],
                )
            )
            leaving[-1].start()
            at += out.shape[0]
    for copy in leaving:
        copy.wait()


def gate_up_kernel(steps, finish, begun, parts, order, *refs):
    count = sum(len(shapes) for shapes, _ in steps)
    blocks, refs = refs[:count], refs[count:]
    gate, up, inverse_gain = refs[:3]
    refs = refs[3:]
    before, refs = (refs[:3], refs[3:]) if begun else ((), refs)
    if finish:
        row_of, down_weight, out = refs[:3]
        parts, refs = refs[3 : 3 + parts], refs[3 + parts :]
        gate_sum, up_sum, square_sum, down_held, down_made, down_in, down_out = refs[:7]
        refs = refs[7:]
    else:
        sums_out, refs = refs[:3], refs[3:]
        gate_sum, up_sum, square_sum = refs[:3]
        refs = refs[3:]
    held, weights, sems = refs[:count], refs[count : count + 2 * len(steps)], refs[-1]
    carried = refs[count + 2 * len(steps) : -1]

    copies, at, place, sem = [], 0, 0, 0
    for step, (shapes, column) in enumerate(steps):
        mine = []
        for shape in shapes:
            mine.append(pltpu.make_async_copy(blocks[at], held[at], sems.at[sem]))
            at, sem = at + 1, sem + 1
        width = shapes[0][2]
        for index in range(sum(shape[0] for shape in shapes)):
            for source, target in ((gate, weights[2 * step]), (up, weights[2 * step + 1])):
                mine.append(
                    pltpu.make_async_copy(
                        source.at[order[place], pl.ds(column, width)],
                        target.at[pl.ds(index * width, width)],
                        sems.at[sem],
                    )
                )
                sem += 1
            place += 1
        copies.append(mine)
    last = []
    for source, target in zip(before, carried):
        last.append(pltpu.make_async_copy(source, target, sems.at[sem]))
        sem += 1
    down_copies = down_reads(down_weight, down_held, down_in, 0) if finish else []
    for mine in [*copies, last, down_copies]:
        for copy in mine:
            copy.start()
    total = jnp.zeros(square_sum.shape, F32)
    lanes = square_sum.shape[1]
    at, place = 0, 0
    for step, (shapes, column) in enumerate(steps):
        for copy in copies[step]:
            copy.wait()
        pieces = []
        width = shapes[0][2]
        for shape in shapes:
            for index in range(shape[0]):
                pieces.append(held[at][index])
            at += 1
        block = jnp.concatenate(pieces, axis=1)
        gate_term = jnp.dot(block, weights[2 * step][...], preferred_element_type=F32)
        gate_sum[...] = gate_sum[...] + gate_term if step > 0 else gate_term
        up_term = jnp.dot(block, weights[2 * step + 1][...], preferred_element_type=F32)
        up_sum[...] = up_sum[...] + up_term if step > 0 else up_term
        for piece in pieces:
            inverse = inverse_gain[order[place]][:, column : column + width]
            plain = piece.astype(F32) * inverse
            squares = plain * plain
            for lane in range(0, width, lanes):
                total = total + squares[:, lane : lane + lanes]
            place += 1
    if begun:
        for copy in last:
            copy.wait()
        gate_sum[...] = gate_sum[...] + carried[0][...]
        up_sum[...] = up_sum[...] + carried[1][...]
        total = total + carried[2][...]
    if not finish:
        square_sum[...] = total
        leaving = [
            pltpu.make_async_copy(source, target, sems.at[sem - 3 + index])
            for index, (source, target) in enumerate(
                zip((gate_sum, up_sum, square_sum), sums_out)
            )
        ]
        for copy in leaving:
            copy.start()
        for copy in leaving:
            copy.wait()
    else:
        features = 6144
        mean_square = jnp.sum(total, axis=1, keepdims=True) / features
        factor = lax.rsqrt(mean_square + 1e-05)
        gate_act = gate_sum[...] * factor
        up_act = up_sum[...] * factor
        hidden = (gate_act * jax.nn.sigmoid(gate_act) * up_act).astype(BF)
        rows = hidden.shape[0]
        places = lax.broadcasted_iota(jnp.int32, (rows, rows), 1)
        picks = jnp.where(places == row_of[...], 1.0, 0.0).astype(BF)
        left = jnp.dot(picks, hidden, preferred_element_type=F32).astype(BF)
        out[...] = left
        down_products(left, down_copies, down_held, down_made, down_out, parts)


def gate_up(order, steps, gate, up, inverse_gain, sums=None, row_of=None, product=None):
    blocks = [block for group, _ in steps for block in group]
    rows, hidden = blocks[0].shape[1], gate.shape[2]
    shapes = tuple((tuple(block.shape for block in group), column) for group, column in steps)
    finish, begun = row_of is not None, sums is not None
    any_place = pl.BlockSpec(memory_space=pl.ANY)
    whole = pl.BlockSpec(memory_space=pltpu.VMEM)
    sum_shapes = [(rows, hidden), (rows, hidden), (rows, 128)]
    operands = [order, *blocks, gate, up, inverse_gain]
    specs = [pl.BlockSpec(memory_space=pltpu.SMEM)] + [any_place] * (len(blocks) + 2) + [whole]
    if begun:
        operands += [in_hbm(array) for array in sums]
        specs += [any_place] * 3
    scratch = []
    if finish:
        weight, wide, parts = product
        operands += [row_of, weight]
        specs += [whole, any_place]
        out_shape = [jax.ShapeDtypeStruct((rows, hidden), BF)]
        out_shape += [pltpu.HBM((part, wide), BF) for part in parts]
        out_specs = [whole] + [any_place] * len(parts)
        scratch += [pltpu.VMEM(shape, F32) for shape in sum_shapes]
        scratch += down_scratch(rows, hidden, wide, len(parts))
    else:
        out_shape = [pltpu.HBM(shape, F32) for shape in sum_shapes]
        out_specs = [any_place] * 3
        scratch += [pltpu.VMEM(shape, F32) for shape in sum_shapes]
    scratch += [pltpu.VMEM(block.shape, BF) for block in blocks]
    depth, copies = 0, len(blocks)
    for group, _ in steps:
        places = sum(block.shape[0] for block in group)
        scratch += [pltpu.VMEM((places * group[0].shape[2], hidden), BF)] * 2
        depth += places * group[0].shape[2]
        copies += 2 * places
    if begun:
        scratch += [pltpu.VMEM(shape, F32) for shape in sum_shapes]
        copies += 3
    scratch.append(pltpu.SemaphoreType.DMA((copies,)))
    return pl.pallas_call(
        lambda *refs: gate_up_kernel(shapes, finish, begun, len(product[2]) if product else 0, *refs),
        out_shape=out_shape,
        in_specs=specs,
        out_specs=out_specs,
        scratch_shapes=scratch,
        compiler_params=pltpu.CompilerParams(vmem_limit_bytes=48 * 2**20),
        cost_estimate=pl.CostEstimate(
            flops=4 * rows * depth * hidden,
            bytes_accessed=2 * depth * (rows + 2 * hidden),
            transcendentals=0,
        ),
    )(*operands)


def down_kernel(start, hidden, weight, *refs):
    outs, (held, made, sems, out_sems) = refs[:-4], refs[-4:]
    copies = down_reads(weight, held, sems, start)
    for copy in copies:
        copy.start()
    down_products(hidden[...], copies, held, made, out_sems, outs)


def down(hidden, weight, start, wide, parts):
    rows, depth = hidden.shape
    any_place = pl.BlockSpec(memory_space=pl.ANY)
    return pl.pallas_call(
        lambda *refs: down_kernel(start, *refs),
        out_shape=[pltpu.HBM((part, wide), BF) for part in parts],
        in_specs=[pl.BlockSpec(memory_space=pltpu.VMEM), any_place],
        out_specs=[any_place] * len(parts),
        scratch_shapes=down_scratch(rows, depth, wide, len(parts)),
        compiler_params=pltpu.CompilerParams(vmem_limit_bytes=24 * 2**20),
        cost_estimate=pl.CostEstimate(
            flops=2 * rows * depth * wide, bytes_accessed=8 * 2**20, transcendentals=0
        ),
    )(hidden, weight)


def add(*terms):
    total = terms[0].astype(F32)
    for term in terms[1:]:
        total = total + term.astype(F32)
    return total.astype(BF)


def send_far(low, high):
    return send(low, True, 1), send(high, True, -1)


def far_sum(came, plus, minus, own):
    low_came, high_came = came
    half = low_came.shape[0]
    plus = lax.dynamic_update_slice_in_dim(plus, add(plus[:half], low_came), 0, 0)
    minus = lax.dynamic_update_slice_in_dim(minus, add(minus[half:], high_came), half, 0)
    return add(own, send(plus, True, 1), send(minus, True, -1))


def near_sum(blocks):
    came = [send(blocks[at], False, step) for at, step in enumerate(FAR_FIRST[:3])]
    return add(blocks[3], *came)


def attend_kernel(first_head, patch, *refs):
    sources, out, held, sems = refs[:4], refs[4], refs[5:9], refs[9]
    copies = [
        pltpu.make_async_copy(source, target, sems.at[index])
        for index, (source, target) in enumerate(zip(sources, held))
    ]
    for copy in copies:
        copy.start()
    for copy in copies:
        copy.wait()
    query, key, value, clean = held
    length, width = query.shape
    scale = 1.0 / math.sqrt(HEAD_SIZE)
    places = lax.broadcasted_iota(jnp.int32, (length, length), 0)
    causal = places >= lax.broadcasted_iota(jnp.int32, (length, length), 1)
    cuts = [slice(at, at + HEAD_SIZE) for at in range(0, width, HEAD_SIZE)]
    scores = [
        lax.dot_general(query[:, cut], key[...], (((1,), (1,)), ((), ())), preferred_element_type=F32)
        for cut in cuts
    ]
    scores = [jnp.where(causal, score * scale, -jnp.inf) for score in scores]
    raised = [jnp.exp(score - jnp.max(score, axis=1, keepdims=True)) for score in scores]
    probs = [(row / jnp.sum(row, axis=1, keepdims=True)).astype(BF) for row in raised]
    attended = [jnp.dot(prob, value[...], preferred_element_type=F32).astype(BF) for prob in probs]
    for head, cut in enumerate(cuts):
        chosen = patch[0, 0] == first_head[0] + head
        for index in range(1, patch.shape[1]):
            chosen = chosen | (patch[0, index] == first_head[0] + head)
        out[:, cut] = jnp.where(chosen, clean[:, cut], attended[head])


def attend(queries, key_states, corrupted_value_state, clean_heads, patch_heads):
    arrays = [array[0] for array in (queries, key_states, corrupted_value_state, clean_heads)]
    length, width = arrays[0].shape
    first_head = (lax.axis_index("head") * (width // HEAD_SIZE)).reshape(1)
    small = pl.BlockSpec(memory_space=pltpu.SMEM)
    return pl.pallas_call(
        attend_kernel,
        out_shape=jax.ShapeDtypeStruct((length, width), BF),
        in_specs=[small, small] + [pl.BlockSpec(memory_space=pl.ANY)] * 4,
        out_specs=pl.BlockSpec(memory_space=pltpu.VMEM),
        scratch_shapes=[pltpu.VMEM(array.shape, BF) for array in arrays]
        + [pltpu.SemaphoreType.DMA((4,))],
        compiler_params=pltpu.CompilerParams(vmem_limit_bytes=8 * 2**20),
        cost_estimate=pl.CostEstimate(
            flops=4 * length * length * width, bytes_accessed=2**20, transcendentals=0
        ),
    )(first_head, patch_heads, *(in_hbm(array) for array in arrays))


def per_device(
    queries,
    key_states,
    corrupted_value_state,
    clean_heads,
    patch_heads,
    out_weight,
    residual,
    norm_gain,
    expert_ids,
    route_weights,
    gate_weight,
    up_weight,
    down_weight,
):
    heads, experts = lax.axis_size("head"), lax.axis_size("expert")
    e_index = lax.axis_index("expert")
    z_index, y_index = e_index // RING, e_index % RING
    first_core = lax.axis_index("head") % 2 == 0
    near_index, far_index = (
        jnp.where(first_core, z_index, y_index),
        jnp.where(first_core, y_index, z_index),
    )
    tokens, width = residual.shape[1], residual.shape[2]
    top = expert_ids.shape[2]
    capacity = 3 * tokens * top // (2 * heads)
    columns = width // experts

    def place_of(near, far):
        return jnp.where(first_core, near * RING + far, far * RING + near)

    weight_all = lax.all_gather(out_weight, "head", axis=0)
    merged = attend(queries, key_states, corrupted_value_state, clean_heads, patch_heads)
    merged = merged.reshape(heads, tokens, merged.shape[1])
    merged = lax.all_to_all(merged, "head", split_axis=0, concat_axis=0, tiled=True)
    pieces, _ = gather_pieces(merged, direct=True)
    first_up, weight_all = lax.optimization_barrier((pieces[2], weight_all))
    pieces = (*pieces[:2], first_up, *pieces[3:])
    pieces = (*pieces, *forward(pieces[2], pieces[5]))

    pairs = expert_ids.reshape(-1)
    onehot = (pairs[:, None] == jnp.arange(heads)[None, :]).astype(F32)
    earlier = (jnp.arange(pairs.shape[0])[:, None] > jnp.arange(pairs.shape[0])[None, :]).astype(F32)
    ranks = jnp.sum(onehot * jnp.dot(earlier, onehot), axis=1).astype(jnp.int32)
    ranks = ranks.reshape(tokens, top)

    resid = residual[0]
    resid_blocks = resid.reshape(tokens, experts, columns).transpose(1, 0, 2)
    id_block = jnp.concatenate([expert_ids[0], ranks], axis=1).astype(BF)
    id_block = jnp.pad(id_block, ((0, 0), (0, 128 - 2 * top)))
    payload = jnp.concatenate(
        [resid_blocks, jnp.broadcast_to(id_block[None], (experts, tokens, 128))], axis=2
    )
    payload = lax.all_to_all(payload, "expert", split_axis=0, concat_axis=0, tiled=True)
    marks = payload[:, :, columns : columns + 2 * top].astype(jnp.int32)
    prompts = jnp.arange(experts)
    targets = (marks[..., :top] * experts + prompts[:, None, None]) * capacity + marks[..., top:]
    targets = targets.reshape(-1, top).T

    near_steps = jnp.array(PIECE_NEAR)
    far_steps = jnp.array(PIECE_FAR)[:, None]
    order = place_of((near_index + near_steps) % RING, (far_index + far_steps) % RING).reshape(-1)
    at = jnp.arange(experts)
    place = jnp.sum(jnp.where(order[None, :] == at[:, None], at[None, :], 0), axis=1)

    own_gain = lax.dynamic_slice(norm_gain, (e_index * columns,), (columns,))[None]
    projected, slots = project(
        place, pieces, weight_all, payload, own_gain, targets,
        heads * experts * capacity,
    )
    own_projected = lax.all_to_all(projected, "expert", split_axis=0, concat_axis=0, tiled=True)

    slots = slots.reshape(heads, experts * capacity, columns)
    slots = lax.all_to_all(slots, "head", split_axis=0, concat_axis=0, tiled=True)
    pieces, own_projected = gather_pieces(slots.reshape(-1, columns), after=own_projected)
    first, second, first_up, first_down, second_up, second_down = pieces
    gate = in_hbm(gate_weight[0].reshape(experts, columns, -1))
    up = in_hbm(up_weight[0].reshape(experts, columns, -1))
    inverse_gain = (1.0 / norm_gain).reshape(experts, 1, columns)
    sums = gate_up(
        order[:8], [((block,), 0) for block in (first, second, first_up, first_down)],
        gate, up, inverse_gain,
    )
    second_up, second_down, *sums = lax.optimization_barrier((second_up, second_down, *sums))
    far_first, far_second = forward(first_up, second_down)
    sums = gate_up(
        order[8:12], [((second_up,), 0), ((second_down,), 0)], gate, up, inverse_gain, sums=sums
    )

    steps = jnp.array(FAR_FIRST)
    prompt = place_of(
        (near_index + steps[:, None]) % RING, (far_index + steps[None, :]) % RING
    )[:, :, None, None]
    source = jnp.arange(heads)[None, None, :, None]
    slot = jnp.arange(capacity)[None, None, None, :]
    row_of = ((source * experts + prompt) * capacity + slot).reshape(-1, 1)
    rows = heads * experts * capacity // RING
    parts = (rows // 2, rows // 2, rows, rows, rows)
    weight = in_hbm(down_weight[0])
    wide = width // 2
    hidden, *first_parts = gate_up(
        order[12:], [((far_first,), 0), ((far_second,), 0)], gate, up, inverse_gain, sums=sums,
        row_of=row_of, product=(weight, wide, parts),
    )
    own_slots = expert_ids[0] * capacity + ranks
    first_came = send_far(*first_parts[:2])
    last_parts = down(hidden, weight, wide, width - wide, parts)
    low, high, *first_came = lax.optimization_barrier((*last_parts[:2], *first_came))
    last_came = send_far(low, high)
    total = jnp.concatenate(
        [far_sum(first_came, *first_parts[2:]), far_sum(last_came, *last_parts[2:])], axis=1
    )
    totals = near_sum(total.reshape(RING, -1, width))
    totals = totals.reshape(heads, capacity, width)
    returned = lax.all_to_all(totals, "head", split_axis=0, concat_axis=0, tiled=True)
    returned = returned.reshape(heads * capacity, width)
    own_projected = own_projected.transpose(1, 0, 2).reshape(tokens, width)
    layer_out = residual[0].astype(F32) + own_projected.astype(F32)
    for k in range(top):
        pick = (own_slots[:, k : k + 1] == jnp.arange(heads * capacity)[None, :]).astype(BF)
        picked = jnp.dot(pick, returned, preferred_element_type=F32)
        layer_out = layer_out + picked * route_weights[0][:, k : k + 1]
    return layer_out.astype(BF).reshape(residual.shape)


def solution(mesh):
    placed = (
        P("expert", None, "head"),
        P("expert", None, "head"),
        P("expert", None, "head"),
        P("expert", None, "head"),
        P("expert", None),
        P("head", "expert"),
        P("expert", "head", None),
        P(),
        P("expert", "head", None),
        P("expert", "head", None),
        P("head", None, "expert"),
        P("head", None, "expert"),
        P("head", "expert", None),
    )
    return jax.shard_map(
        per_device, mesh=mesh, in_specs=placed, out_specs=P("expert", "head", None), check_vma=False
    )
```

```python
import math

import jax
import jax.numpy as jnp
from jax import lax
from jax.experimental import pallas as pl
from jax.experimental.pallas import tpu as pltpu
from jax.sharding import PartitionSpec as P

HEAD_SIZE = 128
RING = 4
NEAR_FIRST = (0, -1, 1, 2)
FAR_FIRST = (2, 1, -1, 0)
BF = jnp.bfloat16
F32 = jnp.float32


def ring_pairs(near, step):
    pairs = []
    for head in range(8):
        for z in range(RING):
            for y in range(RING):
                if near == (head % 2 == 0):
                    target = ((z + step) % RING) * RING + y
                else:
                    target = z * RING + (y + step) % RING
                pairs.append((head * 16 + z * RING + y, head * 16 + target))
    return pairs


def send(block, near, step):
    return lax.ppermute(block, ("head", "expert"), ring_pairs(near, step))


def gather_pieces(block, direct=False, after=None):
    half = block.shape[0] // 2
    up = send(block, True, 1)
    down = send(block, True, -1)
    first = jnp.stack([block, up])
    if direct:
        far = send(block, True, 2)
    else:
        far_low = send(up[:half], True, 1)
        far_high = send(down[half:], True, -1)
        if after is not None:
            far_low, far_high, after = lax.optimization_barrier((far_low, far_high, after))
        far = jnp.concatenate([far_low, far_high], axis=0)
    first_up = send(first, False, 1)
    first_down = send(first, False, -1)
    second = jnp.stack([down, far])
    second_up = send(second, False, 1)
    second_down = send(second, False, -1)
    return (first, second, first_up, first_down, second_up, second_down), after


def forward(first_up, second_down):
    return send(first_up, False, 1), send(second_down, False, -1)


PIECE_NEAR = ((0, -1), (1, 2), (0, -1), (0, -1), (1, 2), (1, 2), (0, -1), (1, 2))
PIECE_FAR = (0, 0, -1, 1, -1, 1, 2, 2)


def in_hbm(array):
    return pltpu.with_memory_space_constraint(array, pltpu.HBM)


def project_kernel(place, *refs):
    blocks, (weight, resid, gain, targets, projected, slots, total, rows) = refs[:8], refs[8:]
    count, width = projected.shape[0], projected.shape[2]
    acc = None
    for group in range(weight.shape[0]):
        block = jnp.concatenate([ref[:, group] for ref in blocks], axis=0)
        block = block.reshape(-1, block.shape[-1])
        term = jnp.dot(block, weight[group], preferred_element_type=F32)
        acc = term if acc is None else acc + term
    total[...] = acc.reshape(total.shape)
    for prompt in range(count):
        value = total[place[prompt]]
        projected[prompt] = value.astype(BF)
        hidden = value + resid[prompt][:, :width].astype(F32)
        rows[prompt] = (hidden * gain[...]).astype(BF)
    tokens = rows[...].reshape(-1, width)
    slot_ids = lax.broadcasted_iota(jnp.int32, (slots.shape[0], tokens.shape[0]), 0)
    chosen = (slot_ids == targets[0:1, :]) | (slot_ids == targets[1:2, :])
    dispatch = jnp.where(chosen, 1.0, 0.0).astype(BF)
    slots[...] = jnp.dot(dispatch, tokens, preferred_element_type=F32).astype(BF)


def project(place, blocks, weight, resid, gain, targets, slot_count):
    count, rows = resid.shape[0], resid.shape[1]
    width = weight.shape[2]
    whole = pl.BlockSpec(memory_space=pltpu.VMEM)
    return pl.pallas_call(
        project_kernel,
        out_shape=[
            jax.ShapeDtypeStruct((count, rows, width), BF),
            jax.ShapeDtypeStruct((slot_count, width), BF),
        ],
        in_specs=[pl.BlockSpec(memory_space=pltpu.SMEM)] + [whole] * (len(blocks) + 4),
        out_specs=[whole, whole],
        scratch_shapes=[
            pltpu.VMEM((count, rows, width), F32),
            pltpu.VMEM((count, rows, width), BF),
        ],
        compiler_params=pltpu.CompilerParams(vmem_limit_bytes=24 * 2**20),
        cost_estimate=pl.CostEstimate(
            flops=2 * count * rows * 6144 * width, bytes_accessed=10 * 2**20, transcendentals=0
        ),
    )(place, *blocks, weight, resid, gain, targets)


DOWN_STEP = 1536


def down_scratch(rows, depth, wide, parts):
    chunks = wide // DOWN_STEP
    return [
        pltpu.VMEM((chunks, depth, DOWN_STEP), BF),
        pltpu.VMEM((chunks, rows, DOWN_STEP), BF),
        pltpu.SemaphoreType.DMA((chunks,)),
        pltpu.SemaphoreType.DMA((chunks, parts)),
    ]


def down_reads(weight, held, sems, start):
    return [
        pltpu.make_async_copy(
            weight.at[:, pl.ds(start + chunk * DOWN_STEP, DOWN_STEP)],
            held.at[chunk],
            sems.at[chunk],
        )
        for chunk in range(held.shape[0])
    ]


def down_products(left, copies, held, made, out_sems, outs):
    leaving = []
    for chunk, copy in enumerate(copies):
        copy.wait()
        made[chunk] = jnp.dot(left, held[chunk], preferred_element_type=F32).astype(BF)
        at = 0
        for index, out in enumerate(outs):
            leaving.append(
                pltpu.make_async_copy(
                    made.at[chunk, pl.ds(at, out.shape[0])],
                    out.at[:, pl.ds(chunk * DOWN_STEP, DOWN_STEP)],
                    out_sems.at[chunk, index],
                )
            )
            leaving[-1].start()
            at += out.shape[0]
    for copy in leaving:
        copy.wait()


def gate_up_kernel(steps, finish, begun, parts, order, *refs):
    count = sum(len(shapes) for shapes, _ in steps)
    blocks, refs = refs[:count], refs[count:]
    gate, up, inverse_gain = refs[:3]
    refs = refs[3:]
    before, refs = (refs[:3], refs[3:]) if begun else ((), refs)
    if finish:
        row_of, down_weight, out = refs[:3]
        parts, refs = refs[3 : 3 + parts], refs[3 + parts :]
        gate_sum, up_sum, square_sum, down_held, down_made, down_in, down_out = refs[:7]
        refs = refs[7:]
    else:
        sums_out, refs = refs[:3], refs[3:]
        gate_sum, up_sum, square_sum = refs[:3]
        refs = refs[3:]
    held, weights, sems = refs[:count], refs[count : count + 2 * len(steps)], refs[-1]
    carried = refs[count + 2 * len(steps) : -1]

    copies, at, place, sem = [], 0, 0, 0
    for step, (shapes, column) in enumerate(steps):
        mine = []
        for shape in shapes:
            mine.append(pltpu.make_async_copy(blocks[at], held[at], sems.at[sem]))
            at, sem = at + 1, sem + 1
        width = shapes[0][2]
        for index in range(sum(shape[0] for shape in shapes)):
            for source, target in ((gate, weights[2 * step]), (up, weights[2 * step + 1])):
                mine.append(
                    pltpu.make_async_copy(
                        source.at[order[place], pl.ds(column, width)],
                        target.at[pl.ds(index * width, width)],
                        sems.at[sem],
                    )
                )
                sem += 1
            place += 1
        copies.append(mine)
    last = []
    for source, target in zip(before, carried):
        last.append(pltpu.make_async_copy(source, target, sems.at[sem]))
        sem += 1
    down_copies = down_reads(down_weight, down_held, down_in, 0) if finish else []
    for mine in [*copies, last, down_copies]:
        for copy in mine:
            copy.start()
    total = jnp.zeros(square_sum.shape, F32)
    lanes = square_sum.shape[1]
    at, place = 0, 0
    for step, (shapes, column) in enumerate(steps):
        for copy in copies[step]:
            copy.wait()
        pieces = []
        width = shapes[0][2]
        for shape in shapes:
            for index in range(shape[0]):
                pieces.append(held[at][index])
            at += 1
        block = jnp.concatenate(pieces, axis=1)
        gate_term = jnp.dot(block, weights[2 * step][...], preferred_element_type=F32)
        gate_sum[...] = gate_sum[...] + gate_term if step > 0 else gate_term
        up_term = jnp.dot(block, weights[2 * step + 1][...], preferred_element_type=F32)
        up_sum[...] = up_sum[...] + up_term if step > 0 else up_term
        for piece in pieces:
            inverse = inverse_gain[order[place]][:, column : column + width]
            plain = piece.astype(F32) * inverse
            squares = plain * plain
            for lane in range(0, width, lanes):
                total = total + squares[:, lane : lane + lanes]
            place += 1
    if begun:
        for copy in last:
            copy.wait()
        gate_sum[...] = gate_sum[...] + carried[0][...]
        up_sum[...] = up_sum[...] + carried[1][...]
        total = total + carried[2][...]
    if not finish:
        square_sum[...] = total
        leaving = [
            pltpu.make_async_copy(source, target, sems.at[sem - 3 + index])
            for index, (source, target) in enumerate(
                zip((gate_sum, up_sum, square_sum), sums_out)
            )
        ]
        for copy in leaving:
            copy.start()
        for copy in leaving:
            copy.wait()
    else:
        features = 6144
        mean_square = jnp.sum(total, axis=1, keepdims=True) / features
        factor = lax.rsqrt(mean_square + 1e-05)
        gate_act = gate_sum[...] * factor
        up_act = up_sum[...] * factor
        hidden = (gate_act * jax.nn.sigmoid(gate_act) * up_act).astype(BF)
        rows = hidden.shape[0]
        places = lax.broadcasted_iota(jnp.int32, (rows, rows), 1)
        picks = jnp.where(places == row_of[...], 1.0, 0.0).astype(BF)
        left = jnp.dot(picks, hidden, preferred_element_type=F32).astype(BF)
        out[...] = left
        down_products(left, down_copies, down_held, down_made, down_out, parts)


def gate_up(order, steps, gate, up, inverse_gain, sums=None, row_of=None, product=None):
    blocks = [block for group, _ in steps for block in group]
    rows, hidden = blocks[0].shape[1], gate.shape[2]
    shapes = tuple((tuple(block.shape for block in group), column) for group, column in steps)
    finish, begun = row_of is not None, sums is not None
    any_place = pl.BlockSpec(memory_space=pl.ANY)
    whole = pl.BlockSpec(memory_space=pltpu.VMEM)
    sum_shapes = [(rows, hidden), (rows, hidden), (rows, 128)]
    operands = [order, *blocks, gate, up, inverse_gain]
    specs = [pl.BlockSpec(memory_space=pltpu.SMEM)] + [any_place] * (len(blocks) + 2) + [whole]
    if begun:
        operands += [in_hbm(array) for array in sums]
        specs += [any_place] * 3
    scratch = []
    if finish:
        weight, wide, parts = product
        operands += [row_of, weight]
        specs += [whole, any_place]
        out_shape = [jax.ShapeDtypeStruct((rows, hidden), BF)]
        out_shape += [pltpu.HBM((part, wide), BF) for part in parts]
        out_specs = [whole] + [any_place] * len(parts)
        scratch += [pltpu.VMEM(shape, F32) for shape in sum_shapes]
        scratch += down_scratch(rows, hidden, wide, len(parts))
    else:
        out_shape = [pltpu.HBM(shape, F32) for shape in sum_shapes]
        out_specs = [any_place] * 3
        scratch += [pltpu.VMEM(shape, F32) for shape in sum_shapes]
    scratch += [pltpu.VMEM(block.shape, BF) for block in blocks]
    depth, copies = 0, len(blocks)
    for group, _ in steps:
        places = sum(block.shape[0] for block in group)
        scratch += [pltpu.VMEM((places * group[0].shape[2], hidden), BF)] * 2
        depth += places * group[0].shape[2]
        copies += 2 * places
    if begun:
        scratch += [pltpu.VMEM(shape, F32) for shape in sum_shapes]
        copies += 3
    scratch.append(pltpu.SemaphoreType.DMA((copies,)))
    return pl.pallas_call(
        lambda *refs: gate_up_kernel(shapes, finish, begun, len(product[2]) if product else 0, *refs),
        out_shape=out_shape,
        in_specs=specs,
        out_specs=out_specs,
        scratch_shapes=scratch,
        compiler_params=pltpu.CompilerParams(vmem_limit_bytes=48 * 2**20),
        cost_estimate=pl.CostEstimate(
            flops=4 * rows * depth * hidden,
            bytes_accessed=2 * depth * (rows + 2 * hidden),
            transcendentals=0,
        ),
    )(*operands)


def down_kernel(start, hidden, weight, *refs):
    outs, (held, made, sems, out_sems) = refs[:-4], refs[-4:]
    copies = down_reads(weight, held, sems, start)
    for copy in copies:
        copy.start()
    down_products(hidden[...], copies, held, made, out_sems, outs)


def down(hidden, weight, start, wide, parts):
    rows, depth = hidden.shape
    any_place = pl.BlockSpec(memory_space=pl.ANY)
    return pl.pallas_call(
        lambda *refs: down_kernel(start, *refs),
        out_shape=[pltpu.HBM((part, wide), BF) for part in parts],
        in_specs=[pl.BlockSpec(memory_space=pltpu.VMEM), any_place],
        out_specs=[any_place] * len(parts),
        scratch_shapes=down_scratch(rows, depth, wide, len(parts)),
        compiler_params=pltpu.CompilerParams(vmem_limit_bytes=24 * 2**20),
        cost_estimate=pl.CostEstimate(
            flops=2 * rows * depth * wide, bytes_accessed=8 * 2**20, transcendentals=0
        ),
    )(hidden, weight)


def add(*terms):
    total = terms[0].astype(F32)
    for term in terms[1:]:
        total = total + term.astype(F32)
    return total.astype(BF)


def send_far(low, high):
    return send(low, True, 1), send(high, True, -1)


def far_sum(came, plus, minus, own):
    low_came, high_came = came
    half = low_came.shape[0]
    plus = lax.dynamic_update_slice_in_dim(plus, add(plus[:half], low_came), 0, 0)
    minus = lax.dynamic_update_slice_in_dim(minus, add(minus[half:], high_came), half, 0)
    return add(own, send(plus, True, 1), send(minus, True, -1))


def near_sum(blocks):
    came = [send(blocks[at], False, step) for at, step in enumerate(FAR_FIRST[:3])]
    return add(blocks[3], *came)


def attend_kernel(first_head, patch, *refs):
    sources, out, held, sems = refs[:4], refs[4], refs[5:9], refs[9]
    copies = [
        pltpu.make_async_copy(source, target, sems.at[index])
        for index, (source, target) in enumerate(zip(sources, held))
    ]
    for copy in copies:
        copy.start()
    for copy in copies:
        copy.wait()
    query, key, value, clean = held
    length, width = query.shape
    scale = 1.0 / math.sqrt(HEAD_SIZE)
    places = lax.broadcasted_iota(jnp.int32, (length, length), 0)
    causal = places >= lax.broadcasted_iota(jnp.int32, (length, length), 1)
    cuts = [slice(at, at + HEAD_SIZE) for at in range(0, width, HEAD_SIZE)]
    scores = [
        lax.dot_general(query[:, cut], key[...], (((1,), (1,)), ((), ())), preferred_element_type=F32)
        for cut in cuts
    ]
    scores = [jnp.where(causal, score * scale, -jnp.inf) for score in scores]
    raised = [jnp.exp(score - jnp.max(score, axis=1, keepdims=True)) for score in scores]
    probs = [(row / jnp.sum(row, axis=1, keepdims=True)).astype(BF) for row in raised]
    attended = [jnp.dot(prob, value[...], preferred_element_type=F32).astype(BF) for prob in probs]
    for head, cut in enumerate(cuts):
        chosen = patch[0, 0] == first_head[0] + head
        for index in range(1, patch.shape[1]):
            chosen = chosen | (patch[0, index] == first_head[0] + head)
        out[:, cut] = jnp.where(chosen, clean[:, cut], attended[head])


def attend(queries, key_states, corrupted_value_state, clean_heads, patch_heads):
    arrays = [array[0] for array in (queries, key_states, corrupted_value_state, clean_heads)]
    length, width = arrays[0].shape
    first_head = (lax.axis_index("head") * (width // HEAD_SIZE)).reshape(1)
    small = pl.BlockSpec(memory_space=pltpu.SMEM)
    return pl.pallas_call(
        attend_kernel,
        out_shape=jax.ShapeDtypeStruct((length, width), BF),
        in_specs=[small, small] + [pl.BlockSpec(memory_space=pl.ANY)] * 4,
        out_specs=pl.BlockSpec(memory_space=pltpu.VMEM),
        scratch_shapes=[pltpu.VMEM(array.shape, BF) for array in arrays]
        + [pltpu.SemaphoreType.DMA((4,))],
        compiler_params=pltpu.CompilerParams(vmem_limit_bytes=8 * 2**20),
        cost_estimate=pl.CostEstimate(
            flops=4 * length * length * width, bytes_accessed=2**20, transcendentals=0
        ),
    )(first_head, patch_heads, *(in_hbm(array) for array in arrays))


def per_device(
    queries,
    key_states,
    corrupted_value_state,
    clean_heads,
    patch_heads,
    out_weight,
    residual,
    norm_gain,
    expert_ids,
    route_weights,
    gate_weight,
    up_weight,
    down_weight,
):
    heads, experts = lax.axis_size("head"), lax.axis_size("expert")
    e_index = lax.axis_index("expert")
    z_index, y_index = e_index // RING, e_index % RING
    first_core = lax.axis_index("head") % 2 == 0
    near_index, far_index = (
        jnp.where(first_core, z_index, y_index),
        jnp.where(first_core, y_index, z_index),
    )
    tokens, width = residual.shape[1], residual.shape[2]
    top = expert_ids.shape[2]
    capacity = 3 * tokens * top // (2 * heads)
    columns = width // experts

    def place_of(near, far):
        return jnp.where(first_core, near * RING + far, far * RING + near)

    weight_all = lax.all_gather(out_weight, "head", axis=0)
    merged = attend(queries, key_states, corrupted_value_state, clean_heads, patch_heads)
    merged = merged.reshape(heads, tokens, merged.shape[1])
    merged = lax.all_to_all(merged, "head", split_axis=0, concat_axis=0, tiled=True)
    pieces, _ = gather_pieces(merged, direct=True)
    first_up, weight_all = lax.optimization_barrier((pieces[2], weight_all))
    pieces = (*pieces[:2], first_up, *pieces[3:])
    pieces = (*pieces, *forward(pieces[2], pieces[5]))

    pairs = expert_ids.reshape(-1)
    onehot = (pairs[:, None] == jnp.arange(heads)[None, :]).astype(F32)
    earlier = (jnp.arange(pairs.shape[0])[:, None] > jnp.arange(pairs.shape[0])[None, :]).astype(F32)
    ranks = jnp.sum(onehot * jnp.dot(earlier, onehot), axis=1).astype(jnp.int32)
    ranks = ranks.reshape(tokens, top)

    resid = residual[0]
    resid_blocks = resid.reshape(tokens, experts, columns).transpose(1, 0, 2)
    id_block = jnp.concatenate([expert_ids[0], ranks], axis=1).astype(BF)
    id_block = jnp.pad(id_block, ((0, 0), (0, 128 - 2 * top)))
    payload = jnp.concatenate(
        [resid_blocks, jnp.broadcast_to(id_block[None], (experts, tokens, 128))], axis=2
    )
    payload = lax.all_to_all(payload, "expert", split_axis=0, concat_axis=0, tiled=True)
    marks = payload[:, :, columns : columns + 2 * top].astype(jnp.int32)
    prompts = jnp.arange(experts)
    targets = (marks[..., :top] * experts + prompts[:, None, None]) * capacity + marks[..., top:]
    targets = targets.reshape(-1, top).T

    near_steps = jnp.array(PIECE_NEAR)
    far_steps = jnp.array(PIECE_FAR)[:, None]
    order = place_of((near_index + near_steps) % RING, (far_index + far_steps) % RING).reshape(-1)
    at = jnp.arange(experts)
    place = jnp.sum(jnp.where(order[None, :] == at[:, None], at[None, :], 0), axis=1)

    own_gain = lax.dynamic_slice(norm_gain, (e_index * columns,), (columns,))[None]
    projected, slots = project(
        place, pieces, weight_all, payload, own_gain, targets,
        heads * experts * capacity,
    )
    own_projected = lax.all_to_all(projected, "expert", split_axis=0, concat_axis=0, tiled=True)

    slots = slots.reshape(heads, experts * capacity, columns)
    slots = lax.all_to_all(slots, "head", split_axis=0, concat_axis=0, tiled=True)
    pieces, own_projected = gather_pieces(slots.reshape(-1, columns), after=own_projected)
    first, second, first_up, first_down, second_up, second_down = pieces
    gate = in_hbm(gate_weight[0].reshape(experts, columns, -1))
    up = in_hbm(up_weight[0].reshape(experts, columns, -1))
    inverse_gain = (1.0 / norm_gain).reshape(experts, 1, columns)
    sums = gate_up(
        order[:8], [((block,), 0) for block in (first, second, first_up, first_down)],
        gate, up, inverse_gain,
    )
    second_up, second_down, *sums = lax.optimization_barrier((second_up, second_down, *sums))
    far_first, far_second = forward(first_up, second_down)
    sums = gate_up(
        order[8:12], [((second_up,), 0), ((second_down,), 0)], gate, up, inverse_gain, sums=sums
    )

    steps = jnp.array(FAR_FIRST)
    prompt = place_of(
        (near_index + steps[:, None]) % RING, (far_index + steps[None, :]) % RING
    )[:, :, None, None]
    source = jnp.arange(heads)[None, None, :, None]
    slot = jnp.arange(capacity)[None, None, None, :]
    row_of = ((source * experts + prompt) * capacity + slot).reshape(-1, 1)
    rows = heads * experts * capacity // RING
    parts = (rows // 2, rows // 2, rows, rows, rows)
    weight = in_hbm(down_weight[0])
    wide = width // 2
    hidden, *first_parts = gate_up(
        order[12:], [((far_first,), 0), ((far_second,), 0)], gate, up, inverse_gain, sums=sums,
        row_of=row_of, product=(weight, wide, parts),
    )
    own_slots = expert_ids[0] * capacity + ranks
    first_came = send_far(*first_parts[:2])
    last_parts = down(hidden, weight, wide, width - wide, parts)
    low, high, *first_came = lax.optimization_barrier((*last_parts[:2], *first_came))
    last_came = send_far(low, high)
    total = jnp.concatenate(
        [far_sum(first_came, *first_parts[2:]), far_sum(last_came, *last_parts[2:])], axis=1
    )
    totals = near_sum(total.reshape(RING, -1, width))
    totals = totals.reshape(heads, capacity, width)
    returned = lax.all_to_all(totals, "head", split_axis=0, concat_axis=0, tiled=True)
    returned = returned.reshape(heads * capacity, width)
    own_projected = own_projected.transpose(1, 0, 2).reshape(tokens, width)
    layer_out = residual[0].astype(F32) + own_projected.astype(F32)
    for k in range(top):
        pick = (own_slots[:, k : k + 1] == jnp.arange(heads * capacity)[None, :]).astype(BF)
        picked = jnp.dot(pick, returned, preferred_element_type=F32)
        layer_out = layer_out + picked * route_weights[0][:, k : k + 1]
    return layer_out.astype(BF).reshape(residual.shape)


def solution(mesh):
    placed = (
        P("expert", None, "head"),
        P("expert", None, "head"),
        P("expert", None, "head"),
        P("expert", None, "head"),
        P("expert", None),
        P("head", "expert"),
        P("expert", "head", None),
        P(),
        P("expert", "head", None),
        P("expert", "head", None),
        P("head", None, "expert"),
        P("head", None, "expert"),
        P("head", "expert", None),
    )
    return jax.shard_map(
        per_device, mesh=mesh, in_specs=placed, out_specs=P("expert", "head", None), check_vma=False
    )
```

```python
import math

import jax
import jax.numpy as jnp
from jax import lax
from jax.experimental import pallas as pl
from jax.experimental.pallas import tpu as pltpu
from jax.sharding import PartitionSpec as P

HEAD_SIZE = 128
RING = 4
NEAR_FIRST = (0, -1, 1, 2)
FAR_FIRST = (2, 1, -1, 0)
BF = jnp.bfloat16
F32 = jnp.float32


def ring_pairs(near, step):
    pairs = []
    for head in range(8):
        for z in range(RING):
            for y in range(RING):
                if near == (head % 2 == 0):
                    target = ((z + step) % RING) * RING + y
                else:
                    target = z * RING + (y + step) % RING
                pairs.append((head * 16 + z * RING + y, head * 16 + target))
    return pairs


def send(block, near, step):
    return lax.ppermute(block, ("head", "expert"), ring_pairs(near, step))


def gather_pieces(block, direct=False, after=None):
    half = block.shape[0] // 2
    up = send(block, True, 1)
    down = send(block, True, -1)
    first = jnp.stack([block, up])
    if direct:
        far = send(block, True, 2)
    else:
        far_low = send(up[:half], True, 1)
        far_high = send(down[half:], True, -1)
        if after is not None:
            far_low, far_high, after = lax.optimization_barrier((far_low, far_high, after))
        far = jnp.concatenate([far_low, far_high], axis=0)
    first_up = send(first, False, 1)
    first_down = send(first, False, -1)
    second = jnp.stack([down, far])
    second_up = send(second, False, 1)
    second_down = send(second, False, -1)
    return (first, second, first_up, first_down, second_up, second_down), after


def forward(first_up, second_down):
    return send(first_up, False, 1), send(second_down, False, -1)


PIECE_NEAR = ((0, -1), (1, 2), (0, -1), (0, -1), (1, 2), (1, 2), (0, -1), (1, 2))
PIECE_FAR = (0, 0, -1, 1, -1, 1, 2, 2)


def in_hbm(array):
    return pltpu.with_memory_space_constraint(array, pltpu.HBM)


def project_kernel(place, *refs):
    blocks, (weight, resid, gain, targets, projected, slots, total, rows) = refs[:8], refs[8:]
    count, width = projected.shape[0], projected.shape[2]
    acc = None
    for group in range(weight.shape[0]):
        block = jnp.concatenate([ref[:, group] for ref in blocks], axis=0)
        block = block.reshape(-1, block.shape[-1])
        term = jnp.dot(block, weight[group], preferred_element_type=F32)
        acc = term if acc is None else acc + term
    total[...] = acc.reshape(total.shape)
    for prompt in range(count):
        value = total[place[prompt]]
        projected[prompt] = value.astype(BF)
        hidden = value + resid[prompt][:, :width].astype(F32)
        rows[prompt] = (hidden * gain[...]).astype(BF)
    tokens = rows[...].reshape(-1, width)
    slot_ids = lax.broadcasted_iota(jnp.int32, (slots.shape[0], tokens.shape[0]), 0)
    chosen = (slot_ids == targets[0:1, :]) | (slot_ids == targets[1:2, :])
    dispatch = jnp.where(chosen, 1.0, 0.0).astype(BF)
    slots[...] = jnp.dot(dispatch, tokens, preferred_element_type=F32).astype(BF)


def project(place, blocks, weight, resid, gain, targets, slot_count):
    count, rows = resid.shape[0], resid.shape[1]
    width = weight.shape[2]
    whole = pl.BlockSpec(memory_space=pltpu.VMEM)
    return pl.pallas_call(
        project_kernel,
        out_shape=[
            jax.ShapeDtypeStruct((count, rows, width), BF),
            jax.ShapeDtypeStruct((slot_count, width), BF),
        ],
        in_specs=[pl.BlockSpec(memory_space=pltpu.SMEM)] + [whole] * (len(blocks) + 4),
        out_specs=[whole, whole],
        scratch_shapes=[
            pltpu.VMEM((count, rows, width), F32),
            pltpu.VMEM((count, rows, width), BF),
        ],
        compiler_params=pltpu.CompilerParams(vmem_limit_bytes=24 * 2**20),
        cost_estimate=pl.CostEstimate(
            flops=2 * count * rows * 6144 * width, bytes_accessed=10 * 2**20, transcendentals=0
        ),
    )(place, *blocks, weight, resid, gain, targets)


DOWN_STEP = 1536


def down_scratch(rows, depth, wide, parts):
    chunks = wide // DOWN_STEP
    return [
        pltpu.VMEM((chunks, depth, DOWN_STEP), BF),
        pltpu.VMEM((chunks, rows, DOWN_STEP), BF),
        pltpu.SemaphoreType.DMA((chunks,)),
        pltpu.SemaphoreType.DMA((chunks, parts)),
    ]


def down_reads(weight, held, sems, start):
    return [
        pltpu.make_async_copy(
            weight.at[:, pl.ds(start + chunk * DOWN_STEP, DOWN_STEP)],
            held.at[chunk],
            sems.at[chunk],
        )
        for chunk in range(held.shape[0])
    ]


def down_products(left, copies, held, made, out_sems, outs):
    leaving = []
    for chunk, copy in enumerate(copies):
        copy.wait()
        made[chunk] = jnp.dot(left, held[chunk], preferred_element_type=F32).astype(BF)
        at = 0
        for index, out in enumerate(outs):
            leaving.append(
                pltpu.make_async_copy(
                    made.at[chunk, pl.ds(at, out.shape[0])],
                    out.at[:, pl.ds(chunk * DOWN_STEP, DOWN_STEP)],
                    out_sems.at[chunk, index],
                )
            )
            leaving[-1].start()
            at += out.shape[0]
    for copy in leaving:
        copy.wait()


def gate_up_kernel(steps, finish, begun, parts, order, *refs):
    count = sum(len(shapes) for shapes, _ in steps)
    blocks, refs = refs[:count], refs[count:]
    gate, up, inverse_gain = refs[:3]
    refs = refs[3:]
    before, refs = (refs[:3], refs[3:]) if begun else ((), refs)
    if finish:
        row_of, down_weight, out = refs[:3]
        parts, refs = refs[3 : 3 + parts], refs[3 + parts :]
        gate_sum, up_sum, square_sum, down_held, down_made, down_in, down_out = refs[:7]
        refs = refs[7:]
    else:
        sums_out, refs = refs[:3], refs[3:]
        gate_sum, up_sum, square_sum = refs[:3]
        refs = refs[3:]
    held, weights, sems = refs[:count], refs[count : count + len(steps)], refs[-1]
    carried = refs[count + len(steps) : -1]

    hidden_width = gate.shape[2]
    copies, at, place, sem = [], 0, 0, 0
    for step, (shapes, column) in enumerate(steps):
        mine = []
        for shape in shapes:
            mine.append(pltpu.make_async_copy(blocks[at], held[at], sems.at[sem]))
            at, sem = at + 1, sem + 1
        width = shapes[0][2]
        for index in range(sum(shape[0] for shape in shapes)):
            for part, source in enumerate((gate, up)):
                mine.append(
                    pltpu.make_async_copy(
                        source.at[order[place], pl.ds(column, width)],
                        weights[step].at[
                            pl.ds(index * width, width), pl.ds(part * hidden_width, hidden_width)
                        ],
                        sems.at[sem],
                    )
                )
                sem += 1
            place += 1
        copies.append(mine)
    last = []
    for source, target in zip(before, carried):
        last.append(pltpu.make_async_copy(source, target, sems.at[sem]))
        sem += 1
    down_copies = down_reads(down_weight, down_held, down_in, 0) if finish else []
    for mine in [*copies, last, down_copies]:
        for copy in mine:
            copy.start()
    total = jnp.zeros(square_sum.shape, F32)
    lanes = square_sum.shape[1]
    at, place = 0, 0
    for step, (shapes, column) in enumerate(steps):
        for copy in copies[step]:
            copy.wait()
        pieces = []
        width = shapes[0][2]
        for shape in shapes:
            for index in range(shape[0]):
                pieces.append(held[at][index])
            at += 1
        block = jnp.concatenate(pieces, axis=1)
        both = jnp.dot(block, weights[step][...], preferred_element_type=F32)
        gate_term, up_term = both[:, :hidden_width], both[:, hidden_width:]
        gate_sum[...] = gate_sum[...] + gate_term if step > 0 else gate_term
        up_sum[...] = up_sum[...] + up_term if step > 0 else up_term
        for piece in pieces:
            inverse = inverse_gain[order[place]][:, column : column + width]
            plain = piece.astype(F32) * inverse
            squares = plain * plain
            for lane in range(0, width, lanes):
                total = total + squares[:, lane : lane + lanes]
            place += 1
    if begun:
        for copy in last:
            copy.wait()
        gate_sum[...] = gate_sum[...] + carried[0][...]
        up_sum[...] = up_sum[...] + carried[1][...]
        total = total + carried[2][...]
    if not finish:
        square_sum[...] = total
        leaving = [
            pltpu.make_async_copy(source, target, sems.at[sem - 3 + index])
            for index, (source, target) in enumerate(
                zip((gate_sum, up_sum, square_sum), sums_out)
            )
        ]
        for copy in leaving:
            copy.start()
        for copy in leaving:
            copy.wait()
    else:
        features = 6144
        mean_square = jnp.sum(total, axis=1, keepdims=True) / features
        factor = lax.rsqrt(mean_square + 1e-05)
        gate_act = gate_sum[...] * factor
        up_act = up_sum[...] * factor
        hidden = (gate_act * jax.nn.sigmoid(gate_act) * up_act).astype(BF)
        rows = hidden.shape[0]
        places = lax.broadcasted_iota(jnp.int32, (rows, rows), 1)
        picks = jnp.where(places == row_of[...], 1.0, 0.0).astype(BF)
        left = jnp.dot(picks, hidden, preferred_element_type=F32).astype(BF)
        out[...] = left
        down_products(left, down_copies, down_held, down_made, down_out, parts)


def gate_up(order, steps, gate, up, inverse_gain, sums=None, row_of=None, product=None):
    blocks = [block for group, _ in steps for block in group]
    rows, hidden = blocks[0].shape[1], gate.shape[2]
    shapes = tuple((tuple(block.shape for block in group), column) for group, column in steps)
    finish, begun = row_of is not None, sums is not None
    any_place = pl.BlockSpec(memory_space=pl.ANY)
    whole = pl.BlockSpec(memory_space=pltpu.VMEM)
    sum_shapes = [(rows, hidden), (rows, hidden), (rows, 128)]
    operands = [order, *blocks, gate, up, inverse_gain]
    specs = [pl.BlockSpec(memory_space=pltpu.SMEM)] + [any_place] * (len(blocks) + 2) + [whole]
    if begun:
        operands += [in_hbm(array) for array in sums]
        specs += [any_place] * 3
    scratch = []
    if finish:
        weight, wide, parts = product
        operands += [row_of, weight]
        specs += [whole, any_place]
        out_shape = [jax.ShapeDtypeStruct((rows, hidden), BF)]
        out_shape += [pltpu.HBM((part, wide), BF) for part in parts]
        out_specs = [whole] + [any_place] * len(parts)
        scratch += [pltpu.VMEM(shape, F32) for shape in sum_shapes]
        scratch += down_scratch(rows, hidden, wide, len(parts))
    else:
        out_shape = [pltpu.HBM(shape, F32) for shape in sum_shapes]
        out_specs = [any_place] * 3
        scratch += [pltpu.VMEM(shape, F32) for shape in sum_shapes]
    scratch += [pltpu.VMEM(block.shape, BF) for block in blocks]
    depth, copies = 0, len(blocks)
    for group, _ in steps:
        places = sum(block.shape[0] for block in group)
        scratch.append(pltpu.VMEM((places * group[0].shape[2], 2 * hidden), BF))
        depth += places * group[0].shape[2]
        copies += 2 * places
    if begun:
        scratch += [pltpu.VMEM(shape, F32) for shape in sum_shapes]
        copies += 3
    scratch.append(pltpu.SemaphoreType.DMA((copies,)))
    return pl.pallas_call(
        lambda *refs: gate_up_kernel(shapes, finish, begun, len(product[2]) if product else 0, *refs),
        out_shape=out_shape,
        in_specs=specs,
        out_specs=out_specs,
        scratch_shapes=scratch,
        compiler_params=pltpu.CompilerParams(vmem_limit_bytes=48 * 2**20),
        cost_estimate=pl.CostEstimate(
            flops=4 * rows * depth * hidden,
            bytes_accessed=2 * depth * (rows + 2 * hidden),
            transcendentals=0,
        ),
    )(*operands)


def down_kernel(start, hidden, weight, *refs):
    outs, (held, made, sems, out_sems) = refs[:-4], refs[-4:]
    copies = down_reads(weight, held, sems, start)
    for copy in copies:
        copy.start()
    down_products(hidden[...], copies, held, made, out_sems, outs)


def down(hidden, weight, start, wide, parts):
    rows, depth = hidden.shape
    any_place = pl.BlockSpec(memory_space=pl.ANY)
    return pl.pallas_call(
        lambda *refs: down_kernel(start, *refs),
        out_shape=[pltpu.HBM((part, wide), BF) for part in parts],
        in_specs=[pl.BlockSpec(memory_space=pltpu.VMEM), any_place],
        out_specs=[any_place] * len(parts),
        scratch_shapes=down_scratch(rows, depth, wide, len(parts)),
        compiler_params=pltpu.CompilerParams(vmem_limit_bytes=24 * 2**20),
        cost_estimate=pl.CostEstimate(
            flops=2 * rows * depth * wide, bytes_accessed=8 * 2**20, transcendentals=0
        ),
    )(hidden, weight)


def add(*terms):
    total = terms[0].astype(F32)
    for term in terms[1:]:
        total = total + term.astype(F32)
    return total.astype(BF)


def send_far(low, high):
    return send(low, True, 1), send(high, True, -1)


def far_sum(came, plus, minus, own):
    low_came, high_came = came
    half = low_came.shape[0]
    plus = lax.dynamic_update_slice_in_dim(plus, add(plus[:half], low_came), 0, 0)
    minus = lax.dynamic_update_slice_in_dim(minus, add(minus[half:], high_came), half, 0)
    return add(own, send(plus, True, 1), send(minus, True, -1))


def near_sum(blocks):
    came = [send(blocks[at], False, step) for at, step in enumerate(FAR_FIRST[:3])]
    return add(blocks[3], *came)


def attend_kernel(first_head, patch, *refs):
    sources, out, held, sems = refs[:4], refs[4], refs[5:9], refs[9]
    copies = [
        pltpu.make_async_copy(source, target, sems.at[index])
        for index, (source, target) in enumerate(zip(sources, held))
    ]
    for copy in copies:
        copy.start()
    for copy in copies:
        copy.wait()
    query, key, value, clean = held
    length, width = query.shape
    scale = 1.0 / math.sqrt(HEAD_SIZE)
    places = lax.broadcasted_iota(jnp.int32, (length, length), 0)
    causal = places >= lax.broadcasted_iota(jnp.int32, (length, length), 1)
    cuts = [slice(at, at + HEAD_SIZE) for at in range(0, width, HEAD_SIZE)]
    scores = [
        lax.dot_general(query[:, cut], key[...], (((1,), (1,)), ((), ())), preferred_element_type=F32)
        for cut in cuts
    ]
    scores = [jnp.where(causal, score * scale, -jnp.inf) for score in scores]
    raised = [jnp.exp(score - jnp.max(score, axis=1, keepdims=True)) for score in scores]
    probs = [(row / jnp.sum(row, axis=1, keepdims=True)).astype(BF) for row in raised]
    attended = [jnp.dot(prob, value[...], preferred_element_type=F32).astype(BF) for prob in probs]
    for head, cut in enumerate(cuts):
        chosen = patch[0, 0] == first_head[0] + head
        for index in range(1, patch.shape[1]):
            chosen = chosen | (patch[0, index] == first_head[0] + head)
        out[:, cut] = jnp.where(chosen, clean[:, cut], attended[head])


def attend(queries, key_states, corrupted_value_state, clean_heads, patch_heads):
    arrays = [array[0] for array in (queries, key_states, corrupted_value_state, clean_heads)]
    length, width = arrays[0].shape
    first_head = (lax.axis_index("head") * (width // HEAD_SIZE)).reshape(1)
    small = pl.BlockSpec(memory_space=pltpu.SMEM)
    return pl.pallas_call(
        attend_kernel,
        out_shape=jax.ShapeDtypeStruct((length, width), BF),
        in_specs=[small, small] + [pl.BlockSpec(memory_space=pl.ANY)] * 4,
        out_specs=pl.BlockSpec(memory_space=pltpu.VMEM),
        scratch_shapes=[pltpu.VMEM(array.shape, BF) for array in arrays]
        + [pltpu.SemaphoreType.DMA((4,))],
        compiler_params=pltpu.CompilerParams(vmem_limit_bytes=8 * 2**20),
        cost_estimate=pl.CostEstimate(
            flops=4 * length * length * width, bytes_accessed=2**20, transcendentals=0
        ),
    )(first_head, patch_heads, *(in_hbm(array) for array in arrays))


def per_device(
    queries,
    key_states,
    corrupted_value_state,
    clean_heads,
    patch_heads,
    out_weight,
    residual,
    norm_gain,
    expert_ids,
    route_weights,
    gate_weight,
    up_weight,
    down_weight,
):
    heads, experts = lax.axis_size("head"), lax.axis_size("expert")
    e_index = lax.axis_index("expert")
    z_index, y_index = e_index // RING, e_index % RING
    first_core = lax.axis_index("head") % 2 == 0
    near_index, far_index = (
        jnp.where(first_core, z_index, y_index),
        jnp.where(first_core, y_index, z_index),
    )
    tokens, width = residual.shape[1], residual.shape[2]
    top = expert_ids.shape[2]
    capacity = 3 * tokens * top // (2 * heads)
    columns = width // experts

    def place_of(near, far):
        return jnp.where(first_core, near * RING + far, far * RING + near)

    weight_all = lax.all_gather(out_weight, "head", axis=0)
    merged = attend(queries, key_states, corrupted_value_state, clean_heads, patch_heads)
    merged = merged.reshape(heads, tokens, merged.shape[1])
    merged = lax.all_to_all(merged, "head", split_axis=0, concat_axis=0, tiled=True)
    pieces, _ = gather_pieces(merged, direct=True)
    first_up, weight_all = lax.optimization_barrier((pieces[2], weight_all))
    pieces = (*pieces[:2], first_up, *pieces[3:])
    pieces = (*pieces, *forward(pieces[2], pieces[5]))

    pairs = expert_ids.reshape(-1)
    onehot = (pairs[:, None] == jnp.arange(heads)[None, :]).astype(F32)
    earlier = (jnp.arange(pairs.shape[0])[:, None] > jnp.arange(pairs.shape[0])[None, :]).astype(F32)
    ranks = jnp.sum(onehot * jnp.dot(earlier, onehot), axis=1).astype(jnp.int32)
    ranks = ranks.reshape(tokens, top)

    resid = residual[0]
    resid_blocks = resid.reshape(tokens, experts, columns).transpose(1, 0, 2)
    id_block = jnp.concatenate([expert_ids[0], ranks], axis=1).astype(BF)
    id_block = jnp.pad(id_block, ((0, 0), (0, 128 - 2 * top)))
    payload = jnp.concatenate(
        [resid_blocks, jnp.broadcast_to(id_block[None], (experts, tokens, 128))], axis=2
    )
    payload = lax.all_to_all(payload, "expert", split_axis=0, concat_axis=0, tiled=True)
    marks = payload[:, :, columns : columns + 2 * top].astype(jnp.int32)
    prompts = jnp.arange(experts)
    targets = (marks[..., :top] * experts + prompts[:, None, None]) * capacity + marks[..., top:]
    targets = targets.reshape(-1, top).T

    near_steps = jnp.array(PIECE_NEAR)
    far_steps = jnp.array(PIECE_FAR)[:, None]
    order = place_of((near_index + near_steps) % RING, (far_index + far_steps) % RING).reshape(-1)
    at = jnp.arange(experts)
    place = jnp.sum(jnp.where(order[None, :] == at[:, None], at[None, :], 0), axis=1)

    own_gain = lax.dynamic_slice(norm_gain, (e_index * columns,), (columns,))[None]
    projected, slots = project(
        place, pieces, weight_all, payload, own_gain, targets,
        heads * experts * capacity,
    )
    own_projected = lax.all_to_all(projected, "expert", split_axis=0, concat_axis=0, tiled=True)

    slots = slots.reshape(heads, experts * capacity, columns)
    slots = lax.all_to_all(slots, "head", split_axis=0, concat_axis=0, tiled=True)
    pieces, own_projected = gather_pieces(slots.reshape(-1, columns), after=own_projected)
    first, second, first_up, first_down, second_up, second_down = pieces
    gate = in_hbm(gate_weight[0].reshape(experts, columns, -1))
    up = in_hbm(up_weight[0].reshape(experts, columns, -1))
    inverse_gain = (1.0 / norm_gain).reshape(experts, 1, columns)
    sums = gate_up(
        order[:8], [((block,), 0) for block in (first, second, first_up, first_down)],
        gate, up, inverse_gain,
    )
    second_up, second_down, *sums = lax.optimization_barrier((second_up, second_down, *sums))
    far_first, far_second = forward(first_up, second_down)
    sums = gate_up(
        order[8:12], [((second_up,), 0), ((second_down,), 0)], gate, up, inverse_gain, sums=sums
    )

    steps = jnp.array(FAR_FIRST)
    prompt = place_of(
        (near_index + steps[:, None]) % RING, (far_index + steps[None, :]) % RING
    )[:, :, None, None]
    source = jnp.arange(heads)[None, None, :, None]
    slot = jnp.arange(capacity)[None, None, None, :]
    row_of = ((source * experts + prompt) * capacity + slot).reshape(-1, 1)
    rows = heads * experts * capacity // RING
    parts = (rows // 2, rows // 2, rows, rows, rows)
    weight = in_hbm(down_weight[0])
    wide = width // 2
    hidden, *first_parts = gate_up(
        order[12:], [((far_first,), 0), ((far_second,), 0)], gate, up, inverse_gain, sums=sums,
        row_of=row_of, product=(weight, wide, parts),
    )
    own_slots = expert_ids[0] * capacity + ranks
    first_came = send_far(*first_parts[:2])
    last_parts = down(hidden, weight, wide, width - wide, parts)
    low, high, *first_came = lax.optimization_barrier((*last_parts[:2], *first_came))
    last_came = send_far(low, high)
    total = jnp.concatenate(
        [far_sum(first_came, *first_parts[2:]), far_sum(last_came, *last_parts[2:])], axis=1
    )
    totals = near_sum(total.reshape(RING, -1, width))
    totals = totals.reshape(heads, capacity, width)
    returned = lax.all_to_all(totals, "head", split_axis=0, concat_axis=0, tiled=True)
    returned = returned.reshape(heads * capacity, width)
    own_projected = own_projected.transpose(1, 0, 2).reshape(tokens, width)
    layer_out = residual[0].astype(F32) + own_projected.astype(F32)
    for k in range(top):
        pick = (own_slots[:, k : k + 1] == jnp.arange(heads * capacity)[None, :]).astype(BF)
        picked = jnp.dot(pick, returned, preferred_element_type=F32)
        layer_out = layer_out + picked * route_weights[0][:, k : k + 1]
    return layer_out.astype(BF).reshape(residual.shape)


def solution(mesh):
    placed = (
        P("expert", None, "head"),
        P("expert", None, "head"),
        P("expert", None, "head"),
        P("expert", None, "head"),
        P("expert", None),
        P("head", "expert"),
        P("expert", "head", None),
        P(),
        P("expert", "head", None),
        P("expert", "head", None),
        P("head", None, "expert"),
        P("head", None, "expert"),
        P("head", "expert", None),
    )
    return jax.shard_map(
        per_device, mesh=mesh, in_specs=placed, out_specs=P("expert", "head", None), check_vma=False
    )
```
